32 devices in a mesh: rep: 2 (over y), grp: 4 (over z), tp: 4 (over x, core).
Axes of the slice: x: 2, y: 2, z: 4, core: 2. Of those that a mesh axis runs over, the one named last changes fastest.
Arguments:
- activations: bfloat16 [6, 32, 20, 8192], P('rep', 'grp', None, 'tp'), parts along dimension 0, may hold values from -6 to 6
- cotangent: bfloat16 [6, 32, 20, 8192], P('rep', 'grp', None, 'tp'), parts along dimension 0, may hold values from -6 to 6
- frozen_weight_matrix: bfloat16 [8192, 8192], P('tp'), may hold values from -0.0625 to 0.0625
- adapter_down_weights: bfloat16 [64, 8192, 128], P(('rep', 'grp'), 'tp'), parts along dimension 0, may hold values from -0.5 to 0.5
- adapter_up_weights: bfloat16 [64, 128, 8192], P(('rep', 'grp'), None, 'tp'), parts along dimension 0, may hold values from -0.0625 to 0.0625
- window_adapter: int32 [6, 32], P('rep', 'grp'), parts along dimension 0, may hold values from 0 to 31, as said below
- window_live_rows: int32 [6, 32], P('rep', 'grp'), parts along dimension 0, may hold values from 1 to 20, as said below
- rank_per_adapter: int32 [64], P('rep'), parts along dimension 0, may hold values from 16 to 128, as said below
- slot_per_adapter: int32 [64], P('rep'), parts along dimension 0, may hold values from 0 to 31, as said below
Outputs:
- input_grad: bfloat16 [6, 32, 20, 8192], P('rep', 'grp', None, 'tp'), parts along dimension 0
- grad_down: bfloat16 [64, 8192, 128], P(('rep', 'grp'), 'tp'), parts along dimension 0
- grad_up: bfloat16 [64, 128, 8192], P(('rep', 'grp'), None, 'tp'), parts along dimension 0
The draws below stay inside these ranges and needn't reach their ends.
There are 2 independent parts, one for each index of `rep`. The reference program is written for one: setup_inputs(seed, part) draws one part's arguments, and reference() takes and returns one part's arrays. A program takes and returns all parts, laid end to end along the dimension named above; an argument that names none is the same for every part. Nothing has to cross between parts.
Inputs may be any that keep to these rules, and one draw needn't show every extreme that they name: `window_adapter`: in each microstep, at most 2 of one group's 8 windows name adapters whose slots lie in one owner group's block of 8 slots (owner = slot_per_adapter[a] // 8); in every microstep some owner group gets exactly 2 windows from every group. `window_live_rows`: the first of each group's 8 windows in a microstep has all rows live. `rank_per_adapter`: each rank is 128 divided by 8, 4, 2 or 1, and each of these values is held by a quarter of the 32 adapters. `slot_per_adapter`: A permutation of the 32 slots.
All inputs are finite; a program needn't handle non-finite values. Where the reference program divides by a largest or mean magnitude, that divisor is 1e-20 or more.
Results may differ from the reference program's by a relative error of at most 0.0051.
Values may be sent and summed in bfloat16 or wider, within the bound.
No kernel may reach another device: no remote copies, remote signals or barrier semaphores. Data moves between devices by JAX's collectives and lax.ppermute only.
A program may use at most 192 MiB of HBM per device.

```python
import jax
import jax.numpy as jnp
from jax import lax

MODEL_WIDTH = 8192
ADAPTER_COUNT = 32
LARGEST_RANK = 128
MICRO = 3
SEQ_G = 8
WINDOWS_PER_OWNER = 2
PIECE = 20
PIECES = 32
E_G = 8
N_GRP = 4


def slot_table(key):
    return jax.random.permutation(key, ADAPTER_COUNT).astype(jnp.int32)


def draw_slot_per_adapter(key, part):
    shared = slot_table(key)
    return shared


def draw_rank_per_adapter(key, part):
    key = jax.random.fold_in(key, 2)
    levels = LARGEST_RANK // 8 * jnp.array([1, 2, 4, 8], jnp.int32)
    repeated = jnp.tile(levels, ADAPTER_COUNT // 4)
    return jax.random.permutation(key, repeated).astype(jnp.int32)


def block_owners(key, hottest):
    first_key, second_key = jax.random.split(key)
    others = jnp.arange((N_GRP - 1) * WINDOWS_PER_OWNER, dtype=jnp.int32) // WINDOWS_PER_OWNER
    others = others + (others >= hottest).astype(jnp.int32)
    shuffled = jax.random.permutation(first_key, others)[:SEQ_G - 2]
    owners = jnp.concatenate([jnp.stack([hottest, hottest]).astype(jnp.int32), shuffled])
    return jax.random.permutation(second_key, owners)


def draw_window_adapter(key, part):
    shared = slot_table(key)
    key = jax.random.fold_in(key, 3)
    inverse = jnp.zeros((ADAPTER_COUNT,), jnp.int32).at[shared].set(jnp.arange(ADAPTER_COUNT, dtype=jnp.int32))
    hot_key, block_key, local_key = jax.random.split(key, 3)
    hottest = jax.random.randint(hot_key, (MICRO,), 0, N_GRP).astype(jnp.int32)
    block_keys = jax.random.split(block_key, MICRO * N_GRP)
    owners = jax.vmap(block_owners)(block_keys, jnp.repeat(hottest, N_GRP))
    local_slot = jax.random.randint(local_key, (MICRO, PIECES), 0, E_G).astype(jnp.int32)
    return inverse[owners.reshape(MICRO, PIECES) * E_G + local_slot].astype(jnp.int32)


def draw_window_live_rows(key, part):
    key = jax.random.fold_in(key, 4)
    counts = jax.random.randint(key, (MICRO, PIECES), 1, PIECE + 1)
    leading = (jnp.arange(PIECES) % SEQ_G == 0)[None, :]
    return jnp.where(leading, PIECE, counts).astype(jnp.int32)


def shard_levels(rng, shape, cuts, low, high):
    def one(axis_at, shards_of):
        steps = jax.random.uniform(jax.random.fold_in(jax.random.fold_in(rng, 6), axis_at), (shards_of,), jnp.float32, low / len(cuts), high / len(cuts))
        return jnp.repeat(jnp.exp(steps), shape[axis_at] // shards_of).reshape((-1,) + (1,) * (len(shape) - axis_at - 1))

    factor_of = one(*cuts[0])
    for cut in cuts[1:]:
        factor_of = factor_of * one(*cut)
    return factor_of


def gaussian(own_key, extent, scale, reach, shards=(), kind=jnp.bfloat16):
    gain = shard_levels(own_key, extent, shards, -0.22, 0.18) if shards else 1.0
    values = jax.random.normal(own_key, extent, jnp.float32) * scale * gain
    return jnp.minimum(jnp.maximum(values, -reach), reach).astype(kind)


def setup_inputs(seed: int = 0, part: int = 0) -> dict:
    splits = jax.random.split(jax.random.key(seed), 10)
    part_keys = jax.random.split(jax.random.fold_in(splits[9], part), 10)
    activations = gaussian(part_keys[0], (MICRO, PIECES, PIECE, MODEL_WIDTH), 1.0, 6.0, ((1, 4), (3, 4)))
    cotangent = gaussian(part_keys[1], (MICRO, PIECES, PIECE, MODEL_WIDTH), 1.0, 6.0, ((1, 4), (3, 4)))
    frozen_weight_matrix = gaussian(splits[2], (MODEL_WIDTH, MODEL_WIDTH), MODEL_WIDTH ** -0.5, 0.0625, ((0, 4),))
    adapter_down_weights = gaussian(part_keys[3], (ADAPTER_COUNT, MODEL_WIDTH, LARGEST_RANK), LARGEST_RANK ** -0.5, 0.5, ((0, 4), (1, 4)))
    adapter_up_weights = gaussian(part_keys[4], (ADAPTER_COUNT, LARGEST_RANK, MODEL_WIDTH), MODEL_WIDTH ** -0.5, 0.0625, ((0, 4), (2, 4)))
    window_adapter = draw_window_adapter(jax.random.fold_in(jax.random.fold_in(splits[9], part), 71), part)
    window_live_rows = draw_window_live_rows(jax.random.fold_in(jax.random.fold_in(splits[9], part), 71), part)
    rank_per_adapter = draw_rank_per_adapter(jax.random.fold_in(jax.random.fold_in(splits[9], part), 71), part)
    slot_per_adapter = draw_slot_per_adapter(jax.random.fold_in(jax.random.fold_in(splits[9], part), 71), part)
    return {"activations": activations, "cotangent": cotangent, "frozen_weight_matrix": frozen_weight_matrix, "adapter_down_weights": adapter_down_weights, "adapter_up_weights": adapter_up_weights, "window_adapter": window_adapter, "window_live_rows": window_live_rows, "rank_per_adapter": rank_per_adapter, "slot_per_adapter": slot_per_adapter}


grad_limit = 4.0


def reference(activations, cotangent, frozen_weight_matrix, adapter_down_weights, adapter_up_weights, window_adapter, window_live_rows, rank_per_adapter, slot_per_adapter):
    live_rows = (jnp.arange(PIECE)[None, None, :] < window_live_rows[:, :, None]).astype(jnp.bfloat16)
    masked = cotangent * live_rows[:, :, :, None]
    flat_masked = masked.reshape(MICRO * PIECES * PIECE, MODEL_WIDTH)
    frozen_weight_gradient = jnp.dot(flat_masked, frozen_weight_matrix.T, preferred_element_type=jnp.float32)
    scale_base = LARGEST_RANK // 8
    flat_acts = activations.reshape(MICRO * PIECES, PIECE, MODEL_WIDTH)
    flat_cot = masked.reshape(MICRO * PIECES, PIECE, MODEL_WIDTH)
    flat_ids = window_adapter.reshape(MICRO * PIECES)

    def one_piece(carry, inputs):
        down_gradient_total, up_gradient_total = carry
        rows_in, cot_in, adapter = inputs
        table_slot_index = slot_per_adapter[adapter]
        rank_value = rank_per_adapter[adapter]
        scale = scale_base / rank_value.astype(jnp.float32)
        lane_scale = jnp.where(jnp.arange(LARGEST_RANK) < rank_value, scale, 0.0).astype(jnp.float32)
        down_adapter_matrix = adapter_down_weights[table_slot_index]
        up_adapter_matrix = adapter_up_weights[table_slot_index]
        lifted = (jnp.dot(rows_in, down_adapter_matrix, preferred_element_type=jnp.float32) * lane_scale[None, :]).astype(jnp.bfloat16)
        lowered_program = (jnp.dot(cot_in, up_adapter_matrix.T, preferred_element_type=jnp.float32) * lane_scale[None, :]).astype(jnp.bfloat16)
        down_gradient_total = down_gradient_total.at[table_slot_index].add(jnp.dot(rows_in.T, lowered_program, preferred_element_type=jnp.float32))
        up_gradient_total = up_gradient_total.at[table_slot_index].add(jnp.dot(lifted.T, cot_in, preferred_element_type=jnp.float32))
        adapter_backward = jnp.dot(lowered_program, down_adapter_matrix.T, preferred_element_type=jnp.float32).astype(jnp.bfloat16)
        return (down_gradient_total, up_gradient_total), adapter_backward

    start_carry = (jnp.zeros((ADAPTER_COUNT, MODEL_WIDTH, LARGEST_RANK), jnp.float32), jnp.zeros((ADAPTER_COUNT, LARGEST_RANK, MODEL_WIDTH), jnp.float32))
    (down_gradient_total, up_gradient_total), returns = lax.scan(one_piece, start_carry, (flat_acts, flat_cot, flat_ids))
    summed = frozen_weight_gradient.reshape(MICRO, PIECES, PIECE, MODEL_WIDTH) + returns.reshape(MICRO, PIECES, PIECE, MODEL_WIDTH).astype(jnp.float32)
    input_grad = summed.astype(jnp.bfloat16)
    largest = jnp.maximum(jnp.max(jnp.abs(down_gradient_total)), jnp.max(jnp.abs(up_gradient_total)))
    factor = grad_limit / jnp.maximum(largest, grad_limit)
    grad_down = (down_gradient_total * factor).astype(jnp.bfloat16)
    grad_up = (up_gradient_total * factor).astype(jnp.bfloat16)
    return input_grad, grad_down, grad_up
```

```python
import functools

import jax
import jax.numpy as jnp
from jax import lax
from jax.experimental import pallas as pl
from jax.experimental.pallas import tpu as pltpu
from jax.sharding import PartitionSpec as P

WINDOWS_PER_OWNER = 2

grad_limit = 4.0

BF16 = jnp.bfloat16
F32 = jnp.float32
VMEM_LIMIT = 48 * 1024 * 1024
SMEM_SPEC = pl.BlockSpec(memory_space=pltpu.SMEM)


def params(grid_rank=1):
    return pltpu.CompilerParams(
        dimension_semantics=("arbitrary",) * grid_rank, vmem_limit_bytes=VMEM_LIMIT
    )


def cost(flops, moved):
    return pl.CostEstimate(flops=int(flops), bytes_accessed=int(moved), transcendentals=0)


def feature_block(features, wanted=512):
    return wanted if features % wanted == 0 else features


def window_order(adapter_ref, slot_ref, order_ref, count_ref, groups, slots):
    micro, windows = adapter_ref.shape
    for m in range(micro):
        for o in range(groups):
            count_ref[o] = 0
            for k in range(WINDOWS_PER_OWNER):
                order_ref[(m * groups + o) * WINDOWS_PER_OWNER + k] = -1
        for j in range(windows):
            owner = lax.div(slot_ref[adapter_ref[m, j]], slots)
            k = jnp.minimum(count_ref[owner], WINDOWS_PER_OWNER - 1)
            order_ref[(m * groups + owner) * WINDOWS_PER_OWNER + k] = j
            count_ref[owner] = k + 1


def pack_body(groups, slots, masking, me_ref, adapter_ref, slot_ref, live_ref, x_ref, *rest):
    out_refs = rest[:groups]
    order_ref, count_ref, rows_ref = rest[-3:]
    micro, windows, piece, width = x_ref.shape

    @pl.when(pl.program_id(0) == 0)
    def _():
        window_order(adapter_ref, slot_ref, order_ref, count_ref, groups, slots)

    row = lax.broadcasted_iota(jnp.int32, (piece, width), 0)
    for s in range(groups):
        owner = lax.rem(me_ref[0] + s, groups)
        for m in range(micro):
            for k in range(WINDOWS_PER_OWNER):
                j = order_ref[(m * groups + owner) * WINDOWS_PER_OWNER + k]
                at = jnp.maximum(j, 0)
                values = x_ref[m, at].astype(F32)
                if masking:
                    live = jnp.where(j >= 0, live_ref[m, at], 0)
                    values = jnp.where(row < live, values, 0.0)
                first = (m * WINDOWS_PER_OWNER + k) * piece
                rows_ref[first : first + piece, :] = values
        out_refs[s][...] = rows_ref[...].astype(BF16)


def pack(x, me, adapter, slot_per_adapter, live, groups, slots, masking):
    micro, windows, piece, features = x.shape
    rows = micro * WINDOWS_PER_OWNER * piece
    fb = feature_block(features)
    return pl.pallas_call(
        functools.partial(pack_body, groups, slots, masking),
        grid=(features // fb,),
        out_shape=[jax.ShapeDtypeStruct((rows, features), BF16)] * groups,
        in_specs=[SMEM_SPEC] * 4
        + [pl.BlockSpec((micro, windows, piece, fb), lambda f: (0, 0, 0, f))],
        out_specs=[pl.BlockSpec((rows, fb), lambda f: (0, f))] * groups,
        scratch_shapes=[
            pltpu.SMEM((micro * groups * WINDOWS_PER_OWNER,), jnp.int32),
            pltpu.SMEM((groups,), jnp.int32),
            pltpu.VMEM((rows, fb), F32),
        ],
        compiler_params=params(),
        cost_estimate=cost(0, 2 * x.size * 2),
    )(me, adapter, slot_per_adapter, live, x)


def flat_body(live_ref, x_ref, out_ref, rows_ref):
    micro, windows, piece, width = x_ref.shape
    row = lax.broadcasted_iota(jnp.int32, (piece, width), 0)
    for m in range(micro):
        for j in range(windows):
            first = (m * windows + j) * piece
            rows_ref[first : first + piece, :] = jnp.where(
                row < live_ref[m, j], x_ref[m, j].astype(F32), 0.0
            )
    out_ref[...] = rows_ref[...].astype(BF16)


def flat(x, live):
    micro, windows, piece, features = x.shape
    rows = micro * windows * piece
    fb = feature_block(features)
    return pl.pallas_call(
        flat_body,
        grid=(features // fb,),
        out_shape=jax.ShapeDtypeStruct((rows, features), BF16),
        in_specs=[
            SMEM_SPEC,
            pl.BlockSpec((micro, windows, piece, fb), lambda f: (0, 0, 0, f)),
        ],
        out_specs=pl.BlockSpec((rows, fb), lambda f: (0, f)),
        scratch_shapes=[pltpu.VMEM((rows, fb), F32)],
        compiler_params=params(),
        cost_estimate=cost(0, 2 * x.size * 2),
    )(live, x)


def meta_body(groups, slots, piece, me_ref, slot_ref, rank_ref, *rest):
    adapter_refs = rest[:groups]
    pick_ref, lane_ref, order_ref, count_ref = rest[groups:]
    micro, windows = adapter_refs[0].shape
    top = lane_ref.shape[1]
    column = lax.broadcasted_iota(jnp.int32, (piece, top), 1)
    me = me_ref[0]
    for s in range(groups):
        window_order(adapter_refs[s], slot_ref, order_ref, count_ref, groups, slots)
        for m in range(micro):
            for k in range(WINDOWS_PER_OWNER):
                j = order_ref[(m * groups + me) * WINDOWS_PER_OWNER + k]
                adapter = adapter_refs[s][m, jnp.maximum(j, 0)]
                local = lax.rem(slot_ref[adapter], slots)
                rank = rank_ref[adapter]
                limit = jnp.where(j >= 0, rank, 0)
                wide_rank = jnp.full((piece, top), rank, jnp.int32).astype(F32)
                first = ((s * micro + m) * WINDOWS_PER_OWNER + k) * piece
                lane_ref[first : first + piece, :] = jnp.where(
                    column < limit, (top // 8) / wide_rank, 0.0
                )
                pick_ref[first : first + piece, :] = jnp.full((piece, top), local, jnp.int32)


def meta(me, slot_per_adapter, rank_per_adapter, adapters, slots, piece, top):
    groups = len(adapters)
    micro, windows = adapters[0].shape
    rows = groups * micro * WINDOWS_PER_OWNER * piece
    whole = pl.BlockSpec(memory_space=pltpu.VMEM)
    return pl.pallas_call(
        functools.partial(meta_body, groups, slots, piece),
        out_shape=[
            jax.ShapeDtypeStruct((rows, top), jnp.int32),
            jax.ShapeDtypeStruct((rows, top), F32),
        ],
        in_specs=[SMEM_SPEC] * (3 + groups),
        out_specs=[whole, whole],
        scratch_shapes=[
            pltpu.SMEM((micro * groups * WINDOWS_PER_OWNER,), jnp.int32),
            pltpu.SMEM((groups,), jnp.int32),
        ],
        compiler_params=pltpu.CompilerParams(vmem_limit_bytes=VMEM_LIMIT),
    )(me, slot_per_adapter, rank_per_adapter, *adapters)


def joined(refs):
    return jnp.concatenate([ref[...].astype(F32) for ref in refs], axis=0).astype(BF16)


def project_body(groups, down, pick_ref, *rest):
    row_refs = rest[:groups]
    table_ref, out_ref, rows_ref = rest[groups:]
    step = pl.program_id(0)

    @pl.when(step == 0)
    def _():
        rows_ref[...] = joined(row_refs)
        out_ref[...] = jnp.zeros_like(out_ref)

    together = table_ref.shape[0]
    top = out_ref.shape[1]
    rows = rows_ref[...]
    if down:
        table = jnp.concatenate([table_ref[i] for i in range(together)], axis=1)
        product = jnp.dot(rows, table, preferred_element_type=F32)
    else:
        table = table_ref[...].reshape(together * top, table_ref.shape[2])
        product = lax.dot_general(
            rows, table, (((1,), (1,)), ((), ())), preferred_element_type=F32
        )
    chosen = out_ref[...]
    for i in range(together):
        chosen = jnp.where(
            pick_ref[...] == step * together + i, product[:, i * top : (i + 1) * top], chosen
        )
    out_ref[...] = chosen


def project(row_blocks, pick, table, down):
    groups = len(row_blocks)
    rows, top = pick.shape
    slots = table.shape[0]
    features = row_blocks[0].shape[1]
    together = 2 if slots % 2 == 0 else 1
    whole = pl.BlockSpec(memory_space=pltpu.VMEM)
    return pl.pallas_call(
        functools.partial(project_body, groups, down),
        grid=(slots // together,),
        out_shape=jax.ShapeDtypeStruct((rows, top), F32),
        in_specs=[whole] * (1 + groups)
        + [pl.BlockSpec((together,) + table.shape[1:], lambda e: (e, 0, 0))],
        out_specs=pl.BlockSpec((rows, top), lambda e: (0, 0)),
        scratch_shapes=[pltpu.VMEM((rows, features), BF16)],
        compiler_params=params(),
        cost_estimate=cost(2 * rows * table.size, table.size * 2 + rows * features * 2),
    )(pick, *row_blocks, table)


def spread(values, pick, slots):
    return jnp.concatenate(
        [jnp.where(pick == e, values, 0.0) for e in range(slots)], axis=1
    ).astype(BF16)


def back_body(groups, mine_ref, other_ref, lane_ref, pick_ref, down_ref, *rest):
    out_refs = rest[:groups]
    spread_ref = rest[groups]
    slots, width, top = down_ref.shape

    @pl.when(pl.program_id(0) == 0)
    def _():
        lowered = ((mine_ref[...] + other_ref[...]) * lane_ref[...]).astype(BF16).astype(F32)
        spread_ref[...] = spread(lowered, pick_ref[...], slots)

    table = jnp.concatenate([down_ref[e] for e in range(slots)], axis=1)
    product = lax.dot_general(
        spread_ref[...], table, (((1,), (1,)), ((), ())), preferred_element_type=F32
    )
    rows = out_refs[0].shape[0]
    for s in range(groups):
        out_refs[s][...] = product[s * rows : (s + 1) * rows].astype(BF16)


def back(mine, other, lane, pick, down, groups):
    rows, top = pick.shape
    slots, features, _ = down.shape
    fb = feature_block(features)
    whole = pl.BlockSpec(memory_space=pltpu.VMEM)
    each = rows // groups
    return pl.pallas_call(
        functools.partial(back_body, groups),
        grid=(features // fb,),
        out_shape=[jax.ShapeDtypeStruct((each, features), BF16)] * groups
        + [jax.ShapeDtypeStruct((rows, slots * top), BF16)],
        in_specs=[whole] * 4 + [pl.BlockSpec((slots, fb, top), lambda f: (0, f, 0))],
        out_specs=[pl.BlockSpec((each, fb), lambda f: (0, f))] * groups
        + [pl.BlockSpec((rows, slots * top), lambda f: (0, 0))],
        compiler_params=params(),
        cost_estimate=cost(2 * rows * down.size, down.size * 2 + rows * features * 2),
    )(mine, other, lane, pick, down)


def grads_body(groups, mine_ref, other_ref, lane_ref, pick_ref, low_ref, *rest):
    act_refs = rest[:groups]
    masked_refs = rest[groups : 2 * groups]
    down_ref, up_ref, largest_ref, lift_ref = rest[2 * groups :]
    slots, width, top = down_ref.shape

    @pl.when(pl.program_id(0) == 0)
    def _():
        lifted = ((mine_ref[...] + other_ref[...]) * lane_ref[...]).astype(BF16).astype(F32)
        for e in range(slots):
            part = jnp.where(pick_ref[...] == e, lifted, 0.0)
            lift_ref[e * top : (e + 1) * top, :] = part.T.astype(BF16)
        largest_ref[...] = jnp.zeros_like(largest_ref)

    acts = joined(act_refs)
    masked = joined(masked_refs)
    up = jnp.dot(lift_ref[...], masked, preferred_element_type=F32)
    down = lax.dot_general(
        acts, low_ref[...], (((0,), (0,)), ((), ())), preferred_element_type=F32
    )
    top_up = jnp.zeros((8, width), F32)
    for e in range(slots):
        part = up[e * top : (e + 1) * top]
        up_ref[e] = part
        top_up = jnp.maximum(top_up, jnp.max(jnp.abs(part).reshape(top // 8, 8, width), axis=0))
    top_down = jnp.zeros((8, top), F32)
    for e in range(slots):
        part = down[:, e * top : (e + 1) * top]
        down_ref[e] = part
        top_down = jnp.maximum(
            top_down, jnp.max(jnp.abs(part).reshape(width // 8, 8, top), axis=0)
        )
    for c in range(width // top):
        top_down = jnp.maximum(top_down, top_up[:, c * top : (c + 1) * top])
    largest_ref[...] = jnp.maximum(largest_ref[...], top_down)


def grads(mine, other, lane, pick, low, acts, masked, slots):
    groups = len(acts)
    rows, top = pick.shape
    each, features = acts[0].shape
    fb = feature_block(features)
    whole = pl.BlockSpec(memory_space=pltpu.VMEM)
    return pl.pallas_call(
        functools.partial(grads_body, groups),
        grid=(features // fb,),
        out_shape=[
            jax.ShapeDtypeStruct((slots, features, top), F32),
            jax.ShapeDtypeStruct((slots, top, features), F32),
            jax.ShapeDtypeStruct((8, top), F32),
        ],
        in_specs=[whole] * 5 + [pl.BlockSpec((each, fb), lambda f: (0, f))] * (2 * groups),
        out_specs=[
            pl.BlockSpec((slots, fb, top), lambda f: (0, f, 0)),
            pl.BlockSpec((slots, top, fb), lambda f: (0, 0, f)),
            pl.BlockSpec((8, top), lambda f: (0, 0)),
        ],
        scratch_shapes=[pltpu.VMEM((slots * top, rows), BF16)],
        compiler_params=params(),
        cost_estimate=cost(4 * rows * slots * top * features, 8 * slots * top * features),
    )(mine, other, lane, pick, low, *acts, *masked)


def finish_body(groups, slots, me_ref, adapter_ref, slot_ref, frozen_ref, *rest):
    back_refs = rest[:groups]
    out_ref, count_ref, rows_ref = rest[groups:]
    micro, windows, piece, width = out_ref.shape
    pair = WINDOWS_PER_OWNER * piece
    for s in range(groups):
        for m in range(micro):
            rows_ref[s * micro + m] = back_refs[s][...].astype(F32)[m * pair : (m + 1) * pair]
    for m in range(micro):
        for o in range(groups):
            count_ref[o] = 0
        for j in range(windows):
            owner = lax.div(slot_ref[adapter_ref[m, j]], slots)
            k = count_ref[owner]
            count_ref[owner] = k + 1
            s = lax.rem(owner + groups - me_ref[0], groups)
            both = rows_ref[s * micro + m]
            part = both[:piece]
            for other in range(1, WINDOWS_PER_OWNER):
                part = jnp.where(k == other, both[other * piece : (other + 1) * piece], part)
            first = (m * windows + j) * piece
            out_ref[m, j] = (frozen_ref[first : first + piece, :] + part).astype(BF16)


def finish(me, adapter, slot_per_adapter, frozen, backs, slots, shape):
    groups = len(backs)
    micro, windows, piece, features = shape
    rows, each = frozen.shape[0], backs[0].shape[0]
    fb = feature_block(features)
    return pl.pallas_call(
        functools.partial(finish_body, groups, slots),
        grid=(features // fb,),
        out_shape=jax.ShapeDtypeStruct(shape, BF16),
        in_specs=[SMEM_SPEC] * 3
        + [pl.BlockSpec((rows, fb), lambda f: (0, f))]
        + [pl.BlockSpec((each, fb), lambda f: (0, f))] * groups,
        out_specs=pl.BlockSpec((micro, windows, piece, fb), lambda f: (0, 0, 0, f)),
        scratch_shapes=[
            pltpu.SMEM((groups,), jnp.int32),
            pltpu.VMEM((groups * micro, WINDOWS_PER_OWNER * piece, fb), F32),
        ],
        compiler_params=params(),
        cost_estimate=cost(0, rows * features * 8),
    )(me, adapter, slot_per_adapter, frozen, *backs)


def partner(x, axis, bit):
    count = lax.axis_size(axis)
    return lax.ppermute(x, axis, [(i, i ^ bit) for i in range(count)])


def all_but_last_sum(x, axis):
    count = lax.axis_size(axis)
    bit = 1
    while bit < count:
        other = partner(x, axis, bit)
        if 2 * bit == count:
            return x, other
        x = x + other
        bit *= 2
    return x, jnp.zeros_like(x)


def all_max(x, axis):
    count = lax.axis_size(axis)
    bit = 1
    while bit < count:
        x = jnp.maximum(x, partner(x, axis, bit))
        bit *= 2
    return x


def local(
    activations,
    cotangent,
    frozen_weight_matrix,
    adapter_down_weights,
    adapter_up_weights,
    window_adapter,
    window_live_rows,
    rank_per_adapter,
    slot_per_adapter,
):
    groups = lax.axis_size("grp")
    slots, features, top = adapter_down_weights.shape
    piece = activations.shape[2]
    me = lax.axis_index("grp").astype(jnp.int32).reshape(1)

    def shifted(x, s):
        return lax.ppermute(x, "grp", [(i, (i + s) % groups) for i in range(groups)])

    def to_owners(blocks):
        return [blocks[0]] + [shifted(blocks[s], s) for s in range(1, groups)]

    masked_out = pack(
        cotangent, me, window_adapter, slot_per_adapter, window_live_rows, groups, slots, True
    )
    masked = to_owners(masked_out)
    masked_flat = flat(cotangent, window_live_rows)
    gathered = lax.all_gather(masked_flat, "tp", axis=1, tiled=True)
    adapters = [window_adapter] + [shifted(window_adapter, s) for s in range(1, groups)]
    acts_out = pack(
        activations, me, window_adapter, slot_per_adapter, window_live_rows, groups, slots, False
    )
    acts = to_owners(acts_out)
    pick, lane = meta(
        me, slot_per_adapter, rank_per_adapter, adapters, slots, piece, top
    )
    frozen = lax.dot_general(
        gathered,
        frozen_weight_matrix,
        (((1,), (1,)), ((), ())),
        preferred_element_type=F32,
    )
    low_mine, low_other = all_but_last_sum(
        project(masked, pick, adapter_up_weights, False), "tp"
    )
    *backs, low = back(low_mine, low_other, lane, pick, adapter_down_weights, groups)
    returned = [backs[0]] + [shifted(backs[s], groups - s) for s in range(1, groups)]
    lift_mine, lift_other = all_but_last_sum(
        project(acts, pick, adapter_down_weights, True), "tp"
    )
    down_sum, up_sum, largest = grads(
        lift_mine, lift_other, lane, pick, low, acts, masked, slots
    )
    highest = jnp.max(all_max(all_max(largest, "tp"), "grp"))
    factor = grad_limit / jnp.maximum(highest, grad_limit)
    input_grad = finish(
        me, window_adapter, slot_per_adapter, frozen, returned, slots, activations.shape
    )
    return (
        input_grad,
        (down_sum * factor).astype(BF16),
        (up_sum * factor).astype(BF16),
    )


def solution(mesh):
    return jax.shard_map(
        local,
        mesh=mesh,
        in_specs=(
            P("rep", "grp", None, "tp"),
            P("rep", "grp", None, "tp"),
            P("tp", None),
            P(("rep", "grp"), "tp", None),
            P(("rep", "grp"), None, "tp"),
            P("rep", "grp"),
            P("rep", "grp"),
            P("rep"),
            P("rep"),
        ),
        out_specs=(
            P("rep", "grp", None, "tp"),
            P(("rep", "grp"), "tp", None),
            P(("rep", "grp"), None, "tp"),
        ),
        check_vma=False,
    )
```

```python
import functools

import jax
import jax.numpy as jnp
from jax import lax
from jax.experimental import pallas as pl
from jax.experimental.pallas import tpu as pltpu
from jax.sharding import PartitionSpec as P

WINDOWS_PER_OWNER = 2
NOTES = 8

grad_limit = 4.0

BF16 = jnp.bfloat16
F32 = jnp.float32
VMEM_LIMIT = 60
WHOLE = pl.BlockSpec(memory_space=pltpu.VMEM)
ANY = pl.BlockSpec(memory_space=pl.ANY)


def params(limit=VMEM_LIMIT):
    return pltpu.CompilerParams(
        dimension_semantics=("arbitrary",), vmem_limit_bytes=limit * 1024 * 1024
    )


SMALL = pl.CostEstimate(flops=1000000, bytes_accessed=100000, transcendentals=0)


def feature_block(features, wanted=512):
    return wanted if features % wanted == 0 else features


def window_order(adapter_ref, slot_ref, order_ref, count_ref, groups, slots):
    micro, windows = adapter_ref.shape
    for m in range(micro):
        for o in range(groups):
            count_ref[o] = 0
            for k in range(WINDOWS_PER_OWNER):
                order_ref[(m * groups + o) * WINDOWS_PER_OWNER + k] = -1
        for j in range(windows):
            owner = lax.div(slot_ref[adapter_ref[m, j]], slots)
            k = jnp.minimum(count_ref[owner], WINDOWS_PER_OWNER - 1)
            order_ref[(m * groups + owner) * WINDOWS_PER_OWNER + k] = j
            count_ref[owner] = k + 1


def live_rows_native(live_ref, m, windows):
    sublane = lax.broadcasted_iota(jnp.int32, (windows, 128), 0)
    live = jnp.zeros((windows, 128), jnp.int32)
    for j in range(windows):
        live = jnp.where(sublane == j, live_ref[m, j], live)
    return live


def route_body(
    groups,
    slots,
    piece,
    adapter_in,
    slot_in,
    rank_in,
    live_in,
    x_ref,
    packed_ref,
    flat_ref,
    hot_ref,
    adapter_ref,
    slot_ref,
    rank_ref,
    live_ref,
    arrived,
    order_ref,
    count_ref,
    target_ref,
    alive_ref,
    note_ref,
):
    micro, windows = adapter_ref.shape

    @pl.when(pl.program_id(0) == 0)
    def _():
        copies = [
            pltpu.make_async_copy(there, here, arrived.at[i])
            for i, (there, here) in enumerate(
                (
                    (adapter_in, adapter_ref),
                    (slot_in, slot_ref),
                    (rank_in, rank_ref),
                    (live_in, live_ref),
                )
            )
        ]
        for copy in copies:
            copy.start()
        for copy in copies:
            copy.wait()
        window_order(adapter_ref, slot_ref, order_ref, count_ref, groups, slots)
        row = lax.broadcasted_iota(jnp.int32, (piece, 128), 0)
        note_row = lax.broadcasted_iota(jnp.int32, (NOTES, 128), 0)
        note_column = lax.broadcasted_iota(jnp.int32, (NOTES, 128), 1)
        note_ref[...] = jnp.zeros_like(note_ref)
        for o in range(groups):
            note = jnp.zeros((NOTES, 128), jnp.int32)
            for m in range(micro):
                for k in range(WINDOWS_PER_OWNER):
                    j = order_ref[(m * groups + o) * WINDOWS_PER_OWNER + k]
                    at = jnp.maximum(j, 0)
                    adapter = adapter_ref[m, at]
                    live = jnp.where(j >= 0, live_ref[m, at], 0)
                    limit = jnp.where(j >= 0, rank_ref[adapter], 0)
                    first = ((o * micro + m) * WINDOWS_PER_OWNER + k) * piece
                    target_ref[first : first + piece, :] = jnp.where(
                        row < live, (m * piece + row) * windows + j, -1
                    )
                    value = jnp.where(note_row == 0, lax.rem(slot_ref[adapter], slots), limit)
                    note = jnp.where(note_column == m * WINDOWS_PER_OWNER + k, value, note)
            note_ref[o, :, :128] = note.astype(F32)
        column = lax.broadcasted_iota(jnp.int32, hot_ref.shape, 1)
        hot_ref[...] = jnp.where(column == target_ref[:, :1], 1.0, 0.0).astype(BF16)
        for m in range(micro):
            live = live_rows_native(live_ref, m, windows)
            for p in range(piece):
                first = (m * piece + p) * windows
                alive_ref[first : first + windows, :] = jnp.where(live > p, 1.0, 0.0)

    x = x_ref[...]
    packed = jnp.dot(hot_ref[...], x, preferred_element_type=F32)
    rows = packed.shape[0] // groups
    parts = []
    for o in range(groups):
        parts += [packed[o * rows : (o + 1) * rows], note_ref[o]]
    packed_ref[...] = jnp.concatenate(parts, axis=0).astype(BF16)
    flat_ref[...] = jnp.where(alive_ref[:, :1] > 0.0, x.astype(F32), 0.0).astype(BF16)


def route(x, adapter, slot_per_adapter, rank_per_adapter, live, groups, slots):
    micro, windows = adapter.shape
    native, features = x.shape
    piece = native // (micro * windows)
    rows = groups * micro * WINDOWS_PER_OWNER * piece
    sent = rows + groups * NOTES
    fb = feature_block(features)
    far = pl.BlockSpec(memory_space=pltpu.MemorySpace.HBM)
    return pl.pallas_call(
        functools.partial(route_body, groups, slots, piece),
        grid=(features // fb,),
        out_shape=[
            jax.ShapeDtypeStruct((sent, features), BF16),
            jax.ShapeDtypeStruct((native, features), BF16),
            jax.ShapeDtypeStruct((rows, native), BF16),
        ],
        in_specs=[far] * 4 + [pl.BlockSpec((native, fb), lambda f: (0, f))],
        out_specs=[
            pl.BlockSpec((sent, fb), lambda f: (0, f)),
            pl.BlockSpec((native, fb), lambda f: (0, f)),
            pl.BlockSpec((rows, native), lambda f: (0, 0)),
        ],
        scratch_shapes=[
            pltpu.SMEM(adapter.shape, jnp.int32),
            pltpu.SMEM(slot_per_adapter.shape, jnp.int32),
            pltpu.SMEM(rank_per_adapter.shape, jnp.int32),
            pltpu.SMEM(live.shape, jnp.int32),
            pltpu.SemaphoreType.DMA((4,)),
            pltpu.SMEM((micro * groups * WINDOWS_PER_OWNER,), jnp.int32),
            pltpu.SMEM((groups,), jnp.int32),
            pltpu.VMEM((rows, 128), jnp.int32),
            pltpu.VMEM((native, 128), F32),
            pltpu.VMEM((groups, NOTES, fb), F32),
        ],
        compiler_params=params(),
        cost_estimate=SMALL,
    )(adapter, slot_per_adapter, rank_per_adapter, live, x)


def pack_body(hot_ref, x_ref, out_ref, hot_back_ref):
    @pl.when(pl.program_id(0) == 0)
    def _():
        hot_back_ref[...] = hot_ref[...].astype(F32).T.astype(BF16)

    out_ref[...] = jnp.dot(hot_ref[...], x_ref[...], preferred_element_type=F32).astype(BF16)


def pack(x, hot):
    native, features = x.shape
    rows = hot.shape[0]
    fb = feature_block(features)
    return pl.pallas_call(
        pack_body,
        grid=(features // fb,),
        out_shape=[
            jax.ShapeDtypeStruct((rows, features), BF16),
            jax.ShapeDtypeStruct((native, rows), BF16),
        ],
        in_specs=[WHOLE, pl.BlockSpec((native, fb), lambda f: (0, f))],
        out_specs=[
            pl.BlockSpec((rows, fb), lambda f: (0, f)),
            pl.BlockSpec((native, rows), lambda f: (0, 0)),
        ],
        compiler_params=params(),
        cost_estimate=SMALL,
    )(hot, x)


def frozen_body(parts, more, source_ref, *rest):
    row_refs, weight_refs, out_ref = rest[:parts], rest[parts : 2 * parts], rest[-1]
    total = rest[2 * parts][...] if more else jnp.zeros(out_ref.shape, F32)
    for q in range(parts):
        total += lax.dot_general(
            row_refs[q][...],
            weight_refs[q][...],
            (((1,), (1,)), ((), ())),
            preferred_element_type=F32,
        )
    out_ref[...] = total


def frozen_product(sources, row_blocks, weights, so_far, *after):
    parts = len(row_blocks)
    rows, features = row_blocks[0].shape
    inputs = weights.shape[0]
    nb = 256 if inputs % 256 == 0 else inputs

    def columns(q):
        return pl.BlockSpec((nb, features), lambda n, source: (n, source[q]))

    more = () if so_far is None else (so_far,)
    out_spec = pl.BlockSpec((rows, nb), lambda n, source: (0, n))
    return pl.pallas_call(
        functools.partial(frozen_body, parts, so_far is not None),
        grid_spec=pltpu.PrefetchScalarGridSpec(
            num_scalar_prefetch=1,
            grid=(inputs // nb,),
            in_specs=[WHOLE] * parts
            + [columns(q) for q in range(parts)]
            + [out_spec] * len(more)
            + [ANY] * len(after),
            out_specs=out_spec,
        ),
        out_shape=jax.ShapeDtypeStruct((rows, inputs), F32),
        compiler_params=params(),
        cost_estimate=SMALL,
    )(sources, *row_blocks, *([weights] * parts), *more, *after)


def receive_body(
    groups, windows, piece, sent_ref, table_ref, *rest
):
    out_ref, pick_ref, lane_ref, rows_ref, note_ref = rest[-5:]
    top = out_ref.shape[1]
    count = windows * piece
    together = table_ref.shape[0]
    step = pl.program_id(0)

    @pl.when(step == 0)
    def _():
        sent = sent_ref[...].astype(F32)
        rows_ref[...] = jnp.concatenate(
            [sent[g * (count + NOTES) : g * (count + NOTES) + count] for g in range(groups)], axis=0
        ).astype(BF16)
        column = lax.broadcasted_iota(jnp.int32, (piece, top), 1).astype(F32)
        for g in range(groups):
            first = g * (count + NOTES) + count
            note_ref[...] = sent[first : first + NOTES, :128]
            for at in range(windows):
                limit = note_ref[1:2, at : at + 1]
                first = (g * windows + at) * piece
                lane_ref[first : first + piece, :] = jnp.where(
                    column < limit, (top // 8) / jnp.maximum(limit, 1.0), 0.0
                )
                pick_ref[first : first + piece, :] = jnp.broadcast_to(
                    note_ref[0:1, at : at + 1], (piece, top)
                )
        out_ref[...] = jnp.zeros_like(out_ref)

    table = table_ref[...].reshape(together * top, table_ref.shape[2])
    product = lax.dot_general(
        rows_ref[...], table, (((1,), (1,)), ((), ())), preferred_element_type=F32
    )
    out_ref[...] = choose(pick_ref, product, out_ref[...], step * together, together)


def choose(pick_ref, product, chosen, first, together):
    top = chosen.shape[1]
    for i in range(together):
        here = pick_ref[...] == (first + i).astype(F32)
        chosen = jnp.where(here, product[:, i * top : (i + 1) * top], chosen)
    return chosen


def receive(sent, table, groups, windows, piece, *after):
    slots, top, features = table.shape
    rows = groups * windows * piece
    together = 2 if slots % 2 == 0 else 1
    fixed = pl.BlockSpec((rows, top), lambda e: (0, 0))
    return pl.pallas_call(
        functools.partial(receive_body, groups, windows, piece),
        grid=(slots // together,),
        out_shape=[jax.ShapeDtypeStruct((rows, top), F32)] * 3
        + [jax.ShapeDtypeStruct((rows, features), BF16)],
        in_specs=[WHOLE, pl.BlockSpec((together, top, features), lambda e: (e, 0, 0))]
        + [ANY] * len(after),
        out_specs=[fixed] * 3 + [pl.BlockSpec((rows, features), lambda e: (0, 0))],
        scratch_shapes=[pltpu.VMEM((NOTES, 128), F32)],
        compiler_params=params(),
        cost_estimate=SMALL,
    )(sent, table, *after)


def gate_body(*refs):
    pass


def gate(x, *after):
    return pl.pallas_call(
        gate_body,
        out_shape=jax.ShapeDtypeStruct(x.shape, x.dtype),
        in_specs=[ANY] * (1 + len(after)),
        out_specs=ANY,
        input_output_aliases={0: 0},
        cost_estimate=SMALL,
    )(x, *after)


def project_body(pick_ref, rows_ref, table_ref, *rest):
    out_ref = rest[-1]
    step = pl.program_id(0)
    together = table_ref.shape[0]
    table = jnp.concatenate([table_ref[i] for i in range(together)], axis=1)
    product = jnp.dot(rows_ref[...], table, preferred_element_type=F32)
    chosen = jnp.where(step == 0, jnp.zeros(out_ref.shape, F32), out_ref[...])
    out_ref[...] = choose(pick_ref, product, chosen, step * together, together)


def project(rows, pick, table, *after):
    count, top = pick.shape
    slots = table.shape[0]
    together = 2 if slots % 2 == 0 else 1
    return pl.pallas_call(
        project_body,
        grid=(slots // together,),
        out_shape=jax.ShapeDtypeStruct((count, top), F32),
        in_specs=[
            WHOLE,
            WHOLE,
            pl.BlockSpec((together,) + table.shape[1:], lambda e: (e, 0, 0)),
        ]
        + [ANY] * len(after),
        out_specs=pl.BlockSpec((count, top), lambda e: (0, 0)),
        compiler_params=params(),
        cost_estimate=SMALL,
    )(pick, rows, table, *after)


def spread(values, pick, slots):
    return jnp.concatenate(
        [jnp.where(pick == float(e), values, 0.0) for e in range(slots)], axis=1
    ).astype(BF16)


def back_body(mine_ref, other_ref, lane_ref, pick_ref, down_ref, *rest):
    out_ref, spread_ref = rest[-2:]
    slots, width, top = down_ref.shape

    @pl.when(pl.program_id(0) == 0)
    def _():
        lowered = ((mine_ref[...] + other_ref[...]) * lane_ref[...]).astype(BF16).astype(F32)
        spread_ref[...] = spread(lowered, pick_ref[...], slots)

    table = jnp.concatenate([down_ref[e] for e in range(slots)], axis=1)
    out_ref[...] = lax.dot_general(
        spread_ref[...], table, (((1,), (1,)), ((), ())), preferred_element_type=F32
    ).astype(BF16)


def back(mine, other, lane, pick, down, *after):
    rows, top = pick.shape
    slots, features, _ = down.shape
    fb = feature_block(features)
    return pl.pallas_call(
        back_body,
        grid=(features // fb,),
        out_shape=[
            jax.ShapeDtypeStruct((rows, features), BF16),
            jax.ShapeDtypeStruct((rows, slots * top), BF16),
        ],
        in_specs=[WHOLE] * 4
        + [pl.BlockSpec((slots, fb, top), lambda f: (0, f, 0))]
        + [ANY] * len(after),
        out_specs=[
            pl.BlockSpec((rows, fb), lambda f: (0, f)),
            pl.BlockSpec((rows, slots * top), lambda f: (0, 0)),
        ],
        compiler_params=params(),
        cost_estimate=SMALL,
    )(mine, other, lane, pick, down, *after)


def grads_body(
    slots,
    mine_ref,
    other_ref,
    lane_ref,
    pick_ref,
    low_ref,
    acts_ref,
    masked_ref,
    down_ref,
    up_ref,
    largest_ref,
    lift_ref,
):
    top = lane_ref.shape[1]

    @pl.when(pl.program_id(0) == 0)
    def _():
        lifted = ((mine_ref[...] + other_ref[...]) * lane_ref[...]).astype(BF16).astype(F32)
        for e in range(slots):
            part = jnp.where(pick_ref[...] == float(e), lifted, 0.0)
            lift_ref[e * top : (e + 1) * top, :] = part.T.astype(BF16)
        largest_ref[...] = jnp.zeros_like(largest_ref)

    up = jnp.dot(lift_ref[...], masked_ref[...], preferred_element_type=F32)
    down = lax.dot_general(
        acts_ref[...], low_ref[...], (((0,), (0,)), ((), ())), preferred_element_type=F32
    )
    for e in range(slots):
        up_ref[e] = up[e * top : (e + 1) * top]
        down_ref[e] = down[:, e * top : (e + 1) * top]
    top_up = jnp.max(jnp.abs(up).reshape(slots * top // 8, 8, up.shape[1]), axis=0)
    top_down = jnp.max(jnp.abs(down).reshape(down.shape[0] // 8, 8, slots * top), axis=0)
    largest = largest_ref[...]
    for c in range(up.shape[1] // top):
        largest = jnp.maximum(largest, top_up[:, c * top : (c + 1) * top])
    for e in range(slots):
        largest = jnp.maximum(largest, top_down[:, e * top : (e + 1) * top])
    largest_ref[...] = largest


def grads(mine, other, lane, pick, low, acts, masked, slots):
    rows, top = pick.shape
    features = acts.shape[1]
    fb = feature_block(features)
    return pl.pallas_call(
        functools.partial(grads_body, slots),
        grid=(features // fb,),
        out_shape=[
            jax.ShapeDtypeStruct((slots, features, top), F32),
            jax.ShapeDtypeStruct((slots, top, features), F32),
            jax.ShapeDtypeStruct((8, top), F32),
        ],
        in_specs=[WHOLE] * 5 + [pl.BlockSpec((rows, fb), lambda f: (0, f))] * 2,
        out_specs=[
            pl.BlockSpec((slots, fb, top), lambda f: (0, f, 0)),
            pl.BlockSpec((slots, top, fb), lambda f: (0, 0, f)),
            pl.BlockSpec((8, top), lambda f: (0, 0)),
        ],
        scratch_shapes=[pltpu.VMEM((slots * top, rows), BF16)],
        compiler_params=params(28),
        cost_estimate=SMALL,
    )(mine, other, lane, pick, low, acts, masked)


def scaled_body(largest_ref, down_ref, up_ref, down_out, up_out):
    highest = jnp.max(largest_ref[...], keepdims=True)
    factor = grad_limit / jnp.maximum(highest, grad_limit)
    for e in range(down_ref.shape[0]):
        down_out[e] = (down_ref[e] * factor).astype(BF16)
        up_out[e] = (up_ref[e] * factor).astype(BF16)


def scaled(largest, down, up):
    slots, features, top = down.shape
    down_spec = pl.BlockSpec((1, features, top), lambda e: (e, 0, 0))
    up_spec = pl.BlockSpec((1, top, features), lambda e: (e, 0, 0))
    return pl.pallas_call(
        scaled_body,
        grid=(slots,),
        out_shape=[
            jax.ShapeDtypeStruct(down.shape, BF16),
            jax.ShapeDtypeStruct(up.shape, BF16),
        ],
        in_specs=[WHOLE, down_spec, up_spec],
        out_specs=[down_spec, up_spec],
        compiler_params=params(16),
        cost_estimate=SMALL,
    )(largest, down, up)


def finish_body(hot_ref, frozen_ref, back_ref, out_ref):
    own = jnp.dot(hot_ref[...], back_ref[...], preferred_element_type=F32)
    out_ref[...] = (frozen_ref[...] + own).astype(BF16)


def finish(hot, frozen, returned):
    native, features = frozen.shape
    rows = returned.shape[0]
    fb = feature_block(features)
    return pl.pallas_call(
        finish_body,
        grid=(features // fb,),
        out_shape=jax.ShapeDtypeStruct((native, features), BF16),
        in_specs=[
            WHOLE,
            pl.BlockSpec((native, fb), lambda f: (0, f)),
            pl.BlockSpec((rows, fb), lambda f: (0, f)),
        ],
        out_specs=pl.BlockSpec((native, fb), lambda f: (0, f)),
        compiler_params=params(),
        cost_estimate=SMALL,
    )(hot, frozen, returned)


def partner(x, axis, bit):
    count = lax.axis_size(axis)
    return lax.ppermute(x, axis, [(i, i ^ bit) for i in range(count)])


def all_but_last_sum(x, axis):
    count = lax.axis_size(axis)
    bit = 1
    while bit < count:
        other = partner(x, axis, bit)
        if 2 * bit == count:
            return x, other
        x = x + other
        bit *= 2
    return x, jnp.zeros_like(x)


def gather_rows(x):
    count = lax.axis_size("tp")
    me = lax.axis_index("tp").astype(jnp.int32)
    near = jnp.stack([me, me ^ 1]), [x, partner(x, "tp", 1)]
    sources, blocks = [], []
    for step in range(2, count, 2):
        far = lax.ppermute(x, "tp", [(i, (i + step) % count) for i in range(count)])
        blocks += [far, partner(far, "tp", 1)]
        sources += [(me - step) % count, ((me ^ 1) - step) % count]
    return near, ((jnp.stack(sources), blocks) if blocks else None), blocks[::2]


def all_max(x, axis):
    count = lax.axis_size(axis)
    bit = 1
    while bit < count:
        x = jnp.maximum(x, partner(x, axis, bit))
        bit *= 2
    return x


def local(
    activations,
    cotangent,
    frozen_weight_matrix,
    adapter_down_weights,
    adapter_up_weights,
    window_adapter,
    window_live_rows,
    rank_per_adapter,
    slot_per_adapter,
):
    groups = lax.axis_size("grp")
    slots, features, top = adapter_down_weights.shape
    micro, windows, piece, _ = activations.shape

    def native(x):
        return x.transpose(0, 2, 1, 3).reshape(micro * piece * windows, features)

    def across(x):
        return lax.all_to_all(x, "grp", split_axis=0, concat_axis=0, tiled=True)

    masked_out, masked_flat, hot = route(
        native(cotangent),
        window_adapter,
        slot_per_adapter,
        rank_per_adapter,
        window_live_rows,
        groups,
        slots,
    )
    masked_sent = across(masked_out)
    acts_out, hot_back = pack(native(activations), hot)
    near, far, first_far = gather_rows(masked_flat)
    frozen = frozen_product(*near, frozen_weight_matrix, None)
    acts = across(gate(acts_out, frozen, *first_far))
    low_part, pick, lane, masked = receive(
        masked_sent, adapter_up_weights, groups, micro * WINDOWS_PER_OWNER, piece
    )
    low_mine, low_other = all_but_last_sum(low_part, "tp")
    if far:
        frozen = frozen_product(*far, frozen_weight_matrix, frozen, low_part)
    backs, low = back(low_mine, low_other, lane, pick, adapter_down_weights, frozen)
    returned = across(backs)
    lift_mine, lift_other = all_but_last_sum(
        project(acts, pick, adapter_down_weights, low), "tp"
    )
    down_sum, up_sum, largest = grads(
        lift_mine, lift_other, lane, pick, low, acts, masked, slots
    )
    largest = all_max(all_max(largest, "tp"), "grp")
    grad_down, grad_up = scaled(largest, down_sum, up_sum)
    input_grad = finish(hot_back, frozen, returned)
    return (
        input_grad.reshape(micro, piece, windows, features).transpose(0, 2, 1, 3),
        grad_down,
        grad_up,
    )


def solution(mesh):
    return jax.shard_map(
        local,
        mesh=mesh,
        in_specs=(
            P("rep", "grp", None, "tp"),
            P("rep", "grp", None, "tp"),
            P("tp", None),
            P(("rep", "grp"), "tp", None),
            P(("rep", "grp"), None, "tp"),
            P("rep", "grp"),
            P("rep", "grp"),
            P("rep"),
            P("rep"),
        ),
        out_specs=(
            P("rep", "grp", None, "tp"),
            P(("rep", "grp"), "tp", None),
            P(("rep", "grp"), None, "tp"),
        ),
        check_vma=False,
    )
```

```python
import functools

import jax
import jax.numpy as jnp
from jax import lax
from jax.experimental import pallas as pl
from jax.experimental.pallas import tpu as pltpu
from jax.sharding import PartitionSpec as P

WINDOWS_PER_OWNER = 2
NOTES = 8

grad_limit = 4.0

BF16 = jnp.bfloat16
F32 = jnp.float32
VMEM_LIMIT = 60
WHOLE = pl.BlockSpec(memory_space=pltpu.VMEM)
ANY = pl.BlockSpec(memory_space=pl.ANY)


def params(limit=VMEM_LIMIT):
    return pltpu.CompilerParams(
        dimension_semantics=("arbitrary",), vmem_limit_bytes=limit * 1024 * 1024
    )


SMALL = pl.CostEstimate(flops=1000000, bytes_accessed=100000, transcendentals=0)


def feature_block(features, wanted=512):
    return wanted if features % wanted == 0 else features


def window_order(adapter_ref, slot_ref, order_ref, count_ref, groups, slots):
    micro, windows = adapter_ref.shape
    for m in range(micro):
        for o in range(groups):
            count_ref[o] = 0
            for k in range(WINDOWS_PER_OWNER):
                order_ref[(m * groups + o) * WINDOWS_PER_OWNER + k] = -1
        for j in range(windows):
            owner = lax.div(slot_ref[adapter_ref[m, j]], slots)
            k = jnp.minimum(count_ref[owner], WINDOWS_PER_OWNER - 1)
            order_ref[(m * groups + owner) * WINDOWS_PER_OWNER + k] = j
            count_ref[owner] = k + 1


def live_rows_native(live_ref, m, windows):
    sublane = lax.broadcasted_iota(jnp.int32, (windows, 128), 0)
    live = jnp.zeros((windows, 128), jnp.int32)
    for j in range(windows):
        live = jnp.where(sublane == j, live_ref[m, j], live)
    return live


def route_body(
    groups,
    slots,
    piece,
    adapter_in,
    slot_in,
    rank_in,
    live_in,
    x_ref,
    *rest,
):
    out_refs = rest[:groups]
    (
    flat_ref,
    hot_ref,
    adapter_ref,
    slot_ref,
    rank_ref,
    live_ref,
    arrived,
    order_ref,
    count_ref,
    target_ref,
    alive_ref,
    note_ref,
    packed_ref,
    ) = rest[groups:]
    micro, windows = adapter_ref.shape

    @pl.when(pl.program_id(0) == 0)
    def _():
        copies = [
            pltpu.make_async_copy(there, here, arrived.at[i])
            for i, (there, here) in enumerate(
                (
                    (adapter_in, adapter_ref),
                    (slot_in, slot_ref),
                    (rank_in, rank_ref),
                    (live_in, live_ref),
                )
            )
        ]
        for copy in copies:
            copy.start()
        for copy in copies:
            copy.wait()
        window_order(adapter_ref, slot_ref, order_ref, count_ref, groups, slots)
        row = lax.broadcasted_iota(jnp.int32, (piece, 128), 0)
        note_row = lax.broadcasted_iota(jnp.int32, (NOTES, 128), 0)
        note_column = lax.broadcasted_iota(jnp.int32, (NOTES, 128), 1)
        note_ref[...] = jnp.zeros_like(note_ref)
        for o in range(groups):
            note = jnp.zeros((NOTES, 128), jnp.int32)
            for m in range(micro):
                for k in range(WINDOWS_PER_OWNER):
                    j = order_ref[(m * groups + o) * WINDOWS_PER_OWNER + k]
                    at = jnp.maximum(j, 0)
                    adapter = adapter_ref[m, at]
                    live = jnp.where(j >= 0, live_ref[m, at], 0)
                    limit = jnp.where(j >= 0, rank_ref[adapter], 0)
                    first = ((o * micro + m) * WINDOWS_PER_OWNER + k) * piece
                    target_ref[first : first + piece, :] = jnp.where(
                        row < live, (m * piece + row) * windows + j, -1
                    )
                    value = jnp.where(note_row == 0, lax.rem(slot_ref[adapter], slots), limit)
                    note = jnp.where(note_column == m * WINDOWS_PER_OWNER + k, value, note)
            note_ref[o, :, :128] = note.astype(F32)
        column = lax.broadcasted_iota(jnp.int32, hot_ref.shape, 1)
        hot_ref[...] = jnp.where(column == target_ref[:, :1], 1.0, 0.0).astype(BF16)
        for m in range(micro):
            live = live_rows_native(live_ref, m, windows)
            for p in range(piece):
                first = (m * piece + p) * windows
                alive_ref[first : first + windows, :] = jnp.where(live > p, 1.0, 0.0)

    x = x_ref[...]
    packed = jnp.dot(hot_ref[...], x, preferred_element_type=F32)
    rows = packed.shape[0] // groups
    parts = []
    for o in range(groups):
        parts += [packed[o * rows : (o + 1) * rows], note_ref[o]]
    packed_ref[...] = jnp.concatenate(parts, axis=0)
    for s in range(groups):
        owner = lax.rem(lax.axis_index("grp") + s, groups)
        first = pl.multiple_of(owner * (rows + NOTES), 8)
        out_refs[s][...] = packed_ref[pl.ds(first, rows + NOTES), :].astype(BF16)
    flat_ref[...] = jnp.where(alive_ref[:, :1] > 0.0, x.astype(F32), 0.0).astype(BF16)


def route(x, adapter, slot_per_adapter, rank_per_adapter, live, groups, slots):
    micro, windows = adapter.shape
    native, features = x.shape
    piece = native // (micro * windows)
    rows = groups * micro * WINDOWS_PER_OWNER * piece
    sent = rows // groups + NOTES
    fb = feature_block(features)
    far = pl.BlockSpec(memory_space=pltpu.MemorySpace.HBM)
    return pl.pallas_call(
        functools.partial(route_body, groups, slots, piece),
        grid=(features // fb,),
        out_shape=[jax.ShapeDtypeStruct((sent, features), BF16)] * groups
        + [
            jax.ShapeDtypeStruct((native, features), BF16),
            jax.ShapeDtypeStruct((rows, native), BF16),
        ],
        in_specs=[far] * 4 + [pl.BlockSpec((native, fb), lambda f: (0, f))],
        out_specs=[pl.BlockSpec((sent, fb), lambda f: (0, f))] * groups
        + [
            pl.BlockSpec((native, fb), lambda f: (0, f)),
            pl.BlockSpec((rows, native), lambda f: (0, 0)),
        ],
        scratch_shapes=[
            pltpu.SMEM(adapter.shape, jnp.int32),
            pltpu.SMEM(slot_per_adapter.shape, jnp.int32),
            pltpu.SMEM(rank_per_adapter.shape, jnp.int32),
            pltpu.SMEM(live.shape, jnp.int32),
            pltpu.SemaphoreType.DMA((4,)),
            pltpu.SMEM((micro * groups * WINDOWS_PER_OWNER,), jnp.int32),
            pltpu.SMEM((groups,), jnp.int32),
            pltpu.VMEM((rows, 128), jnp.int32),
            pltpu.VMEM((native, 128), F32),
            pltpu.VMEM((groups, NOTES, fb), F32),
            pltpu.VMEM((groups * sent, fb), F32),
        ],
        compiler_params=params(),
        cost_estimate=SMALL,
    )(adapter, slot_per_adapter, rank_per_adapter, live, x)


def by_shift(out_refs, wide_ref, sign):
    groups = len(out_refs)
    rows = out_refs[0].shape[0]
    for s in range(groups):
        group = lax.rem(lax.axis_index("grp") + groups + sign * s, groups)
        here = pl.ds(pl.multiple_of(group * rows, 8), rows)
        out_refs[s][...] = wide_ref[here, :].astype(BF16)


def by_group(wide_ref, in_refs, sign):
    groups = len(in_refs)
    rows = in_refs[0].shape[0]
    for s in range(groups):
        group = lax.rem(lax.axis_index("grp") + groups + sign * s, groups)
        here = pl.ds(pl.multiple_of(group * rows, 8), rows)
        wide_ref[here, :] = in_refs[s][...].astype(F32)
    return wide_ref[...].astype(BF16)


def pack_body(groups, hot_ref, x_ref, *rest):
    out_refs, hot_back_ref, wide_ref = rest[-2 - groups : -2], rest[-2], rest[-1]

    @pl.when(pl.program_id(0) == 0)
    def _():
        hot_back_ref[...] = hot_ref[...].astype(F32).T.astype(BF16)

    wide_ref[...] = jnp.dot(hot_ref[...], x_ref[...], preferred_element_type=F32)
    by_shift(out_refs, wide_ref, 1)


def pack(x, hot, groups, *after):
    native, features = x.shape
    rows = hot.shape[0]
    fb = feature_block(features)
    return pl.pallas_call(
        functools.partial(pack_body, groups),
        grid=(features // fb,),
        out_shape=[jax.ShapeDtypeStruct((rows // groups, features), BF16)] * groups
        + [jax.ShapeDtypeStruct((native, rows), BF16)],
        in_specs=[WHOLE, pl.BlockSpec((native, fb), lambda f: (0, f))] + [ANY] * len(after),
        out_specs=[pl.BlockSpec((rows // groups, fb), lambda f: (0, f))] * groups
        + [pl.BlockSpec((native, rows), lambda f: (0, 0))],
        scratch_shapes=[pltpu.VMEM((rows, fb), F32)],
        compiler_params=params(),
        cost_estimate=SMALL,
    )(hot, x, *after)


def frozen_body(parts, more, source_ref, *rest):
    row_refs, weight_refs, out_ref = rest[:parts], rest[parts : 2 * parts], rest[-1]
    total = rest[2 * parts][...] if more else jnp.zeros(out_ref.shape, F32)
    for q in range(parts):
        total += lax.dot_general(
            row_refs[q][...],
            weight_refs[q][...],
            (((1,), (1,)), ((), ())),
            preferred_element_type=F32,
        )
    out_ref[...] = total


def frozen_product(sources, row_blocks, weights, so_far, *after):
    parts = len(row_blocks)
    rows, features = row_blocks[0].shape
    inputs = weights.shape[0]
    nb = 512 if inputs % 512 == 0 else inputs

    def columns(q):
        return pl.BlockSpec((nb, features), lambda n, source: (n, source[q]))

    more = () if so_far is None else (so_far,)
    out_spec = pl.BlockSpec((rows, nb), lambda n, source: (0, n))
    return pl.pallas_call(
        functools.partial(frozen_body, parts, so_far is not None),
        grid_spec=pltpu.PrefetchScalarGridSpec(
            num_scalar_prefetch=1,
            grid=(inputs // nb,),
            in_specs=[WHOLE] * parts
            + [columns(q) for q in range(parts)]
            + [out_spec] * len(more)
            + [ANY] * len(after),
            out_specs=out_spec,
        ),
        out_shape=jax.ShapeDtypeStruct((rows, inputs), F32),
        compiler_params=params(),
        cost_estimate=SMALL,
    )(sources, *row_blocks, *([weights] * parts), *more, *after)


def receive_body(groups, windows, piece, table_ref, *rest):
    sent_refs = rest[:groups]
    out_ref, pick_ref, lane_ref, rows_ref, wide_ref, pick_one, lane_one, total_ref = rest[-8:]
    slots, top, _ = table_ref.shape
    count = windows * piece
    step = pl.program_id(0)

    def place(s):
        source = lax.rem(lax.axis_index("grp") + groups - s, groups)
        return pl.ds(pl.multiple_of(source * count, 8), count)

    @pl.when(step == 0)
    def _():
        column = lax.broadcasted_iota(jnp.int32, (piece, top), 1).astype(F32)
        for s in range(groups):
            notes = sent_refs[s][:, :128].astype(F32)[count:]
            for at in range(windows):
                limit = notes[1:2, at : at + 1]
                rows = slice(at * piece, (at + 1) * piece)
                lane_one[rows, :] = jnp.where(
                    column < limit, (top // 8) / jnp.maximum(limit, 1.0), 0.0
                )
                pick_one[rows, :] = jnp.broadcast_to(notes[0:1, at : at + 1], (piece, top))
            lane_ref[place(s), :] = lane_one[...]
            pick_ref[place(s), :] = pick_one[...]
        total_ref[...] = jnp.zeros_like(total_ref)

    for s in range(groups):
        wide_ref[place(s), :] = sent_refs[s][...].astype(F32)[:count]
    rows = wide_ref[...].astype(BF16)
    rows_ref[...] = rows
    total_ref[...] += lax.dot_general(
        rows,
        table_ref[...].reshape(slots * top, table_ref.shape[2]),
        (((1,), (1,)), ((), ())),
        preferred_element_type=F32,
    )

    @pl.when(step == pl.num_programs(0) - 1)
    def _():
        out_ref[...] = choose(pick_ref, total_ref, slots)


def choose(pick_ref, total_ref, slots):
    top = pick_ref.shape[1]
    chosen = total_ref[:, :top]
    for e in range(1, slots):
        chosen = jnp.where(
            pick_ref[...] == float(e), total_ref[:, e * top : (e + 1) * top], chosen
        )
    return chosen


def receive(sent, table, windows, piece, *after):
    groups = len(sent)
    slots, top, features = table.shape
    count = windows * piece
    rows = groups * count
    fb = feature_block(features)
    fixed = pl.BlockSpec((rows, top), lambda f: (0, 0))
    return pl.pallas_call(
        functools.partial(receive_body, groups, windows, piece),
        grid=(features // fb,),
        out_shape=[jax.ShapeDtypeStruct((rows, top), F32)] * 3
        + [jax.ShapeDtypeStruct((rows, features), BF16)],
        in_specs=[pl.BlockSpec((slots, top, fb), lambda f: (0, 0, f))]
        + [pl.BlockSpec((count + NOTES, fb), lambda f: (0, f))] * groups
        + [ANY] * len(after),
        out_specs=[fixed] * 3 + [pl.BlockSpec((rows, fb), lambda f: (0, f))],
        scratch_shapes=[
            pltpu.VMEM((rows, fb), F32),
            pltpu.VMEM((count, top), F32),
            pltpu.VMEM((count, top), F32),
            pltpu.VMEM((rows, slots * top), F32),
        ],
        compiler_params=params(),
        cost_estimate=SMALL,
    )(table, *sent, *after)


def project_body(groups, pick_ref, table_ref, *rest):
    out_ref, rows_ref, wide_ref, total_ref = rest[-4:]
    slots = table_ref.shape[0]
    step = pl.program_id(0)

    @pl.when(step == 0)
    def _():
        total_ref[...] = jnp.zeros_like(total_ref)

    rows = by_group(wide_ref, rest[:groups], -1)
    rows_ref[...] = rows
    table = jnp.concatenate([table_ref[e] for e in range(slots)], axis=1)
    total_ref[...] += jnp.dot(rows, table, preferred_element_type=F32)

    @pl.when(step == pl.num_programs(0) - 1)
    def _():
        out_ref[...] = choose(pick_ref, total_ref, slots)


def project(blocks, pick, table, *after):
    count, top = pick.shape
    groups = len(blocks)
    slots, features = table.shape[:2]
    fb = feature_block(features)
    return pl.pallas_call(
        functools.partial(project_body, groups),
        grid=(features // fb,),
        out_shape=[
            jax.ShapeDtypeStruct((count, top), F32),
            jax.ShapeDtypeStruct((count, features), BF16),
        ],
        in_specs=[WHOLE, pl.BlockSpec((slots, fb, top), lambda f: (0, f, 0))]
        + [pl.BlockSpec((count // groups, fb), lambda f: (0, f))] * groups
        + [ANY] * len(after),
        out_specs=[
            pl.BlockSpec((count, top), lambda f: (0, 0)),
            pl.BlockSpec((count, fb), lambda f: (0, f)),
        ],
        scratch_shapes=[
            pltpu.VMEM((count, fb), F32),
            pltpu.VMEM((count, slots * top), F32),
        ],
        compiler_params=params(),
        cost_estimate=SMALL,
    )(pick, table, *blocks, *after)


def spread(values, pick, slots):
    return jnp.concatenate(
        [jnp.where(pick == float(e), values, 0.0) for e in range(slots)], axis=1
    ).astype(BF16)


def back_body(groups, mine_ref, other_ref, lane_ref, pick_ref, down_ref, *rest):
    out_refs, spread_ref, wide_ref = rest[-2 - groups : -2], rest[-2], rest[-1]
    slots, width, top = down_ref.shape

    @pl.when(pl.program_id(0) == 0)
    def _():
        lowered = ((mine_ref[...] + other_ref[...]) * lane_ref[...]).astype(BF16).astype(F32)
        spread_ref[...] = spread(lowered, pick_ref[...], slots)

    table = jnp.concatenate([down_ref[e] for e in range(slots)], axis=1)
    wide_ref[...] = lax.dot_general(
        spread_ref[...], table, (((1,), (1,)), ((), ())), preferred_element_type=F32
    )
    by_shift(out_refs, wide_ref, -1)


def back(mine, other, lane, pick, down, groups, *after):
    rows, top = pick.shape
    slots, features, _ = down.shape
    fb = feature_block(features)
    each = rows // groups
    return pl.pallas_call(
        functools.partial(back_body, groups),
        grid=(features // fb,),
        out_shape=[jax.ShapeDtypeStruct((each, features), BF16)] * groups
        + [jax.ShapeDtypeStruct((rows, slots * top), BF16)],
        in_specs=[WHOLE] * 4
        + [pl.BlockSpec((slots, fb, top), lambda f: (0, f, 0))]
        + [ANY] * len(after),
        out_specs=[pl.BlockSpec((each, fb), lambda f: (0, f))] * groups
        + [pl.BlockSpec((rows, slots * top), lambda f: (0, 0))],
        scratch_shapes=[pltpu.VMEM((rows, fb), F32)],
        compiler_params=params(),
        cost_estimate=SMALL,
    )(mine, other, lane, pick, down, *after)


def grads_body(
    slots,
    mine_ref,
    other_ref,
    lane_ref,
    pick_ref,
    low_ref,
    acts_ref,
    masked_ref,
    *rest,
):
    down_ref, up_ref, largest_ref, lift_ref = rest[-4:]
    top = lane_ref.shape[1]

    @pl.when(pl.program_id(0) == 0)
    def _():
        lifted = ((mine_ref[...] + other_ref[...]) * lane_ref[...]).astype(BF16).astype(F32)
        for e in range(slots):
            part = jnp.where(pick_ref[...] == float(e), lifted, 0.0)
            lift_ref[e * top : (e + 1) * top, :] = part.T.astype(BF16)
        largest_ref[...] = jnp.zeros_like(largest_ref)

    up = jnp.dot(lift_ref[...], masked_ref[...], preferred_element_type=F32)
    down = lax.dot_general(
        acts_ref[...], low_ref[...], (((0,), (0,)), ((), ())), preferred_element_type=F32
    )
    for e in range(slots):
        up_ref[e] = up[e * top : (e + 1) * top]
        down_ref[e] = down[:, e * top : (e + 1) * top]
    top_up = jnp.max(jnp.abs(up).reshape(slots * top // 8, 8, up.shape[1]), axis=0)
    top_down = jnp.max(jnp.abs(down).reshape(down.shape[0] // 8, 8, slots * top), axis=0)
    largest = largest_ref[...]
    for c in range(up.shape[1] // top):
        largest = jnp.maximum(largest, top_up[:, c * top : (c + 1) * top])
    for e in range(slots):
        largest = jnp.maximum(largest, top_down[:, e * top : (e + 1) * top])
    largest_ref[...] = largest


def grads(mine, other, lane, pick, low, acts, masked, slots, *after):
    rows, top = pick.shape
    features = acts.shape[1]
    fb = feature_block(features)
    return pl.pallas_call(
        functools.partial(grads_body, slots),
        grid=(features // fb,),
        out_shape=[
            jax.ShapeDtypeStruct((slots, features, top), F32),
            jax.ShapeDtypeStruct((slots, top, features), F32),
            jax.ShapeDtypeStruct((8, top), F32),
        ],
        in_specs=[WHOLE] * 5
        + [pl.BlockSpec((rows, fb), lambda f: (0, f))] * 2
        + [ANY] * len(after),
        out_specs=[
            pl.BlockSpec((slots, fb, top), lambda f: (0, f, 0)),
            pl.BlockSpec((slots, top, fb), lambda f: (0, 0, f)),
            pl.BlockSpec((8, top), lambda f: (0, 0)),
        ],
        scratch_shapes=[pltpu.VMEM((slots * top, rows), BF16)],
        compiler_params=params(28),
        cost_estimate=SMALL,
    )(mine, other, lane, pick, low, acts, masked, *after)


def scaled_body(largest_ref, down_ref, up_ref, down_out, up_out):
    highest = jnp.max(largest_ref[...], keepdims=True)
    factor = grad_limit / jnp.maximum(highest, grad_limit)
    for e in range(down_ref.shape[0]):
        down_out[e] = (down_ref[e] * factor).astype(BF16)
        up_out[e] = (up_ref[e] * factor).astype(BF16)


def scaled(largest, down, up):
    slots, features, top = down.shape
    down_spec = pl.BlockSpec((1, features, top), lambda e: (e, 0, 0))
    up_spec = pl.BlockSpec((1, top, features), lambda e: (e, 0, 0))
    return pl.pallas_call(
        scaled_body,
        grid=(slots,),
        out_shape=[
            jax.ShapeDtypeStruct(down.shape, BF16),
            jax.ShapeDtypeStruct(up.shape, BF16),
        ],
        in_specs=[WHOLE, down_spec, up_spec],
        out_specs=[down_spec, up_spec],
        compiler_params=params(16),
        cost_estimate=SMALL,
    )(largest, down, up)


def finish_body(groups, hot_ref, frozen_ref, *rest):
    out_ref, wide_ref = rest[-2:]
    own = jnp.dot(
        hot_ref[...], by_group(wide_ref, rest[:groups], 1), preferred_element_type=F32
    )
    out_ref[...] = (frozen_ref[...] + own).astype(BF16)


def finish(hot, frozen, returned):
    groups = len(returned)
    native, features = frozen.shape
    each = returned[0].shape[0]
    fb = feature_block(features)
    return pl.pallas_call(
        functools.partial(finish_body, groups),
        grid=(features // fb,),
        out_shape=jax.ShapeDtypeStruct((native, features), BF16),
        in_specs=[WHOLE, pl.BlockSpec((native, fb), lambda f: (0, f))]
        + [pl.BlockSpec((each, fb), lambda f: (0, f))] * groups,
        out_specs=pl.BlockSpec((native, fb), lambda f: (0, f)),
        scratch_shapes=[pltpu.VMEM((groups * each, fb), F32)],
        compiler_params=params(),
        cost_estimate=SMALL,
    )(hot, frozen, *returned)


def partner(x, axis, bit):
    count = lax.axis_size(axis)
    return lax.ppermute(x, axis, [(i, i ^ bit) for i in range(count)])


def all_but_last_sum(near_first, x, axis):
    count = lax.axis_size(axis)
    bits = [bit for bit in (1 << i for i in range(count.bit_length())) if bit < count]
    for bit in bits[:-1] if near_first else bits[:0:-1]:
        x = x + partner(x, axis, bit)
    return x, partner(x, axis, bits[-1] if near_first else bits[0])


def gather_rows(x):
    count = lax.axis_size("tp")
    me = lax.axis_index("tp").astype(jnp.int32)
    near = jnp.stack([me, me ^ 1]), [x, partner(x, "tp", 1)]
    sources, blocks = [], []
    for step in range(2, count, 2):
        far = lax.ppermute(x, "tp", [(i, (i + step) % count) for i in range(count)])
        blocks.append(far)
        sources.append((me - step) % count)
    return near, ((jnp.stack(sources), blocks) if blocks else None)


def all_max(x, axis):
    count = lax.axis_size(axis)
    bit = 1
    while bit < count:
        x = jnp.maximum(x, partner(x, axis, bit))
        bit *= 2
    return x


def local(
    activations,
    cotangent,
    frozen_weight_matrix,
    adapter_down_weights,
    adapter_up_weights,
    window_adapter,
    window_live_rows,
    rank_per_adapter,
    slot_per_adapter,
):
    groups = lax.axis_size("grp")
    slots, features, top = adapter_down_weights.shape
    micro, windows, piece, _ = activations.shape

    def native(x):
        return x.transpose(0, 2, 1, 3).reshape(micro * piece * windows, features)

    def across(blocks, sign):
        return [blocks[0]] + [
            lax.ppermute(blocks[s], "grp", [(i, (i + sign * s) % groups) for i in range(groups)])
            for s in range(1, groups)
        ]

    *masked_out, masked_flat, hot = route(
        native(cotangent),
        window_adapter,
        slot_per_adapter,
        rank_per_adapter,
        window_live_rows,
        groups,
        slots,
    )
    masked_sent = across(masked_out, 1)
    near, far = gather_rows(masked_flat)
    frozen = frozen_product(*near, frozen_weight_matrix, None, masked_sent[1])
    *acts_out, hot_back = pack(native(activations), hot, groups, masked_sent[3], frozen)
    acts_sent = across(acts_out, 1)
    low_part, pick, lane, masked = receive(
        masked_sent, adapter_up_weights, micro * WINDOWS_PER_OWNER, piece, frozen
    )

    def lower(near_first, low_part, pick, lane, table, far, weights, frozen):
        low_mine, low_other = all_but_last_sum(near_first, low_part, "tp")
        if far:
            frozen = frozen_product(*far, weights, frozen, low_part)
        *backs, low = back(low_mine, low_other, lane, pick, table, groups, frozen)
        return backs, low, frozen

    def lift(near_first, acts_sent, low, pick, lane, masked, table, far, weights, frozen):
        lift_part, acts = project(acts_sent, pick, table, low)
        lift_mine, lift_other = all_but_last_sum(near_first, lift_part, "tp")
        if far:
            sources, blocks = far
            blocks = [partner(x, "tp", 1) for x in blocks]
            frozen = frozen_product(sources ^ 1, blocks, weights, frozen, lift_part)
        down_sum, up_sum, largest = grads(
            lift_mine, lift_other, lane, pick, low, acts, masked, slots, frozen
        )
        largest = all_max(all_max(largest, "tp"), "grp")
        return scaled(largest, down_sum, up_sum), frozen

    early = window_live_rows[0, 0] <= piece
    backs, low, frozen = lax.cond(
        early,
        functools.partial(lower, True),
        functools.partial(lower, False),
        low_part,
        pick,
        lane,
        adapter_down_weights,
        far,
        frozen_weight_matrix,
        frozen,
    )
    returned = across(backs, -1)
    (grad_down, grad_up), frozen = lax.cond(
        early,
        functools.partial(lift, True),
        functools.partial(lift, False),
        acts_sent,
        low,
        pick,
        lane,
        masked,
        adapter_down_weights,
        far,
        frozen_weight_matrix,
        frozen,
    )
    input_grad = finish(hot_back, frozen, returned)
    return (
        input_grad.reshape(micro, piece, windows, features).transpose(0, 2, 1, 3),
        grad_down,
        grad_up,
    )


def solution(mesh):
    return jax.shard_map(
        local,
        mesh=mesh,
        in_specs=(
            P("rep", "grp", None, "tp"),
            P("rep", "grp", None, "tp"),
            P("tp", None),
            P(("rep", "grp"), "tp", None),
            P(("rep", "grp"), None, "tp"),
            P("rep", "grp"),
            P("rep", "grp"),
            P("rep"),
            P("rep"),
        ),
        out_specs=(
            P("rep", "grp", None, "tp"),
            P(("rep", "grp"), "tp", None),
            P(("rep", "grp"), None, "tp"),
        ),
        check_vma=False,
    )
```

```python
import functools

import jax
import jax.numpy as jnp
from jax import lax
from jax.experimental import pallas as pl
from jax.experimental.pallas import tpu as pltpu
from jax.sharding import PartitionSpec as P

WINDOWS_PER_OWNER = 2
NOTES = 8

grad_limit = 4.0

BF16 = jnp.bfloat16
F32 = jnp.float32
VMEM_LIMIT = 60
WHOLE = pl.BlockSpec(memory_space=pltpu.VMEM)
ANY = pl.BlockSpec(memory_space=pl.ANY)


def params(limit=VMEM_LIMIT):
    return pltpu.CompilerParams(
        dimension_semantics=("arbitrary",), vmem_limit_bytes=limit * 1024 * 1024
    )


SMALL = pl.CostEstimate(flops=1000000, bytes_accessed=100000, transcendentals=0)


def feature_block(features, wanted=512):
    return wanted if features % wanted == 0 else features


def window_order(adapter_ref, slot_ref, order_ref, count_ref, groups, slots):
    micro, windows = adapter_ref.shape
    for m in range(micro):
        for o in range(groups):
            count_ref[o] = 0
            for k in range(WINDOWS_PER_OWNER):
                order_ref[(m * groups + o) * WINDOWS_PER_OWNER + k] = -1
        for j in range(windows):
            owner = lax.div(slot_ref[adapter_ref[m, j]], slots)
            k = jnp.minimum(count_ref[owner], WINDOWS_PER_OWNER - 1)
            order_ref[(m * groups + owner) * WINDOWS_PER_OWNER + k] = j
            count_ref[owner] = k + 1


def live_rows_native(live_ref, m, windows):
    sublane = lax.broadcasted_iota(jnp.int32, (windows, 128), 0)
    live = jnp.zeros((windows, 128), jnp.int32)
    for j in range(windows):
        live = jnp.where(sublane == j, live_ref[m, j], live)
    return live


def route_body(
    groups,
    slots,
    piece,
    adapter_in,
    slot_in,
    rank_in,
    live_in,
    x_ref,
    *rest,
):
    out_refs = rest[:groups]
    (
    flat_ref,
    hot_ref,
    adapter_ref,
    slot_ref,
    rank_ref,
    live_ref,
    arrived,
    order_ref,
    count_ref,
    target_ref,
    alive_ref,
    note_ref,
    packed_ref,
    ) = rest[groups:]
    micro, windows = adapter_ref.shape

    @pl.when(pl.program_id(0) == 0)
    def _():
        copies = [
            pltpu.make_async_copy(there, here, arrived.at[i])
            for i, (there, here) in enumerate(
                (
                    (adapter_in, adapter_ref),
                    (slot_in, slot_ref),
                    (rank_in, rank_ref),
                    (live_in, live_ref),
                )
            )
        ]
        for copy in copies:
            copy.start()
        for copy in copies:
            copy.wait()
        window_order(adapter_ref, slot_ref, order_ref, count_ref, groups, slots)
        row = lax.broadcasted_iota(jnp.int32, (piece, 128), 0)
        note_row = lax.broadcasted_iota(jnp.int32, (NOTES, 128), 0)
        note_column = lax.broadcasted_iota(jnp.int32, (NOTES, 128), 1)
        note_ref[...] = jnp.zeros_like(note_ref)
        for o in range(groups):
            note = jnp.zeros((NOTES, 128), jnp.int32)
            for m in range(micro):
                for k in range(WINDOWS_PER_OWNER):
                    j = order_ref[(m * groups + o) * WINDOWS_PER_OWNER + k]
                    at = jnp.maximum(j, 0)
                    adapter = adapter_ref[m, at]
                    live = jnp.where(j >= 0, live_ref[m, at], 0)
                    limit = jnp.where(j >= 0, rank_ref[adapter], 0)
                    first = ((o * micro + m) * WINDOWS_PER_OWNER + k) * piece
                    target_ref[first : first + piece, :] = jnp.where(
                        row < live, (m * piece + row) * windows + j, -1
                    )
                    value = jnp.where(note_row == 0, lax.rem(slot_ref[adapter], slots), limit)
                    note = jnp.where(note_column == m * WINDOWS_PER_OWNER + k, value, note)
            note_ref[o, :, :128] = note.astype(F32)
        column = lax.broadcasted_iota(jnp.int32, hot_ref.shape, 1)
        hot_ref[...] = jnp.where(column == target_ref[:, :1], 1.0, 0.0).astype(BF16)
        for m in range(micro):
            live = live_rows_native(live_ref, m, windows)
            for p in range(piece):
                first = (m * piece + p) * windows
                alive_ref[first : first + windows, :] = jnp.where(live > p, 1.0, 0.0)

    x = x_ref[...]
    packed = jnp.dot(hot_ref[...], x, preferred_element_type=F32)
    rows = packed.shape[0] // groups
    parts = []
    for o in range(groups):
        parts += [packed[o * rows : (o + 1) * rows], note_ref[o]]
    packed_ref[...] = jnp.concatenate(parts, axis=0)
    for s in range(groups):
        owner = lax.rem(lax.axis_index("grp") + s, groups)
        first = pl.multiple_of(owner * (rows + NOTES), 8)
        out_refs[s][...] = packed_ref[pl.ds(first, rows + NOTES), :].astype(BF16)
    flat_ref[...] = jnp.where(alive_ref[:, :1] > 0.0, x.astype(F32), 0.0).astype(BF16)


def route(x, adapter, slot_per_adapter, rank_per_adapter, live, groups, slots):
    micro, windows = adapter.shape
    native, features = x.shape
    piece = native // (micro * windows)
    rows = groups * micro * WINDOWS_PER_OWNER * piece
    sent = rows // groups + NOTES
    fb = feature_block(features)
    far = pl.BlockSpec(memory_space=pltpu.MemorySpace.HBM)
    return pl.pallas_call(
        functools.partial(route_body, groups, slots, piece),
        grid=(features // fb,),
        out_shape=[jax.ShapeDtypeStruct((sent, features), BF16)] * groups
        + [
            jax.ShapeDtypeStruct((native, features), BF16),
            jax.ShapeDtypeStruct((rows, native), BF16),
        ],
        in_specs=[far] * 4 + [pl.BlockSpec((native, fb), lambda f: (0, f))],
        out_specs=[pl.BlockSpec((sent, fb), lambda f: (0, f))] * groups
        + [
            pl.BlockSpec((native, fb), lambda f: (0, f)),
            pl.BlockSpec((rows, native), lambda f: (0, 0)),
        ],
        scratch_shapes=[
            pltpu.SMEM(adapter.shape, jnp.int32),
            pltpu.SMEM(slot_per_adapter.shape, jnp.int32),
            pltpu.SMEM(rank_per_adapter.shape, jnp.int32),
            pltpu.SMEM(live.shape, jnp.int32),
            pltpu.SemaphoreType.DMA((4,)),
            pltpu.SMEM((micro * groups * WINDOWS_PER_OWNER,), jnp.int32),
            pltpu.SMEM((groups,), jnp.int32),
            pltpu.VMEM((rows, 128), jnp.int32),
            pltpu.VMEM((native, 128), F32),
            pltpu.VMEM((groups, NOTES, fb), F32),
            pltpu.VMEM((groups * sent, fb), F32),
        ],
        compiler_params=params(),
        cost_estimate=SMALL,
    )(adapter, slot_per_adapter, rank_per_adapter, live, x)


def by_shift(out_refs, wide_ref, sign):
    groups = len(out_refs)
    rows = out_refs[0].shape[0]
    for s in range(groups):
        group = lax.rem(lax.axis_index("grp") + groups + sign * s, groups)
        here = pl.ds(pl.multiple_of(group * rows, 8), rows)
        out_refs[s][...] = wide_ref[here, :].astype(BF16)


def by_group(wide_ref, in_refs, sign):
    groups = len(in_refs)
    rows = in_refs[0].shape[0]
    for s in range(groups):
        group = lax.rem(lax.axis_index("grp") + groups + sign * s, groups)
        here = pl.ds(pl.multiple_of(group * rows, 8), rows)
        wide_ref[here, :] = in_refs[s][...].astype(F32)
    return wide_ref[...].astype(BF16)


def pack_body(groups, hot_ref, x_ref, *rest):
    out_refs, hot_back_ref, wide_ref = rest[-2 - groups : -2], rest[-2], rest[-1]

    @pl.when(pl.program_id(0) == 0)
    def _():
        hot_back_ref[...] = hot_ref[...].astype(F32).T.astype(BF16)

    wide_ref[...] = jnp.dot(hot_ref[...], x_ref[...], preferred_element_type=F32)
    by_shift(out_refs, wide_ref, 1)


def pack(x, hot, groups, *after):
    native, features = x.shape
    rows = hot.shape[0]
    fb = feature_block(features)
    return pl.pallas_call(
        functools.partial(pack_body, groups),
        grid=(features // fb,),
        out_shape=[jax.ShapeDtypeStruct((rows // groups, features), BF16)] * groups
        + [jax.ShapeDtypeStruct((native, rows), BF16)],
        in_specs=[WHOLE, pl.BlockSpec((native, fb), lambda f: (0, f))] + [ANY] * len(after),
        out_specs=[pl.BlockSpec((rows // groups, fb), lambda f: (0, f))] * groups
        + [pl.BlockSpec((native, rows), lambda f: (0, 0))],
        scratch_shapes=[pltpu.VMEM((rows, fb), F32)],
        compiler_params=params(),
        cost_estimate=SMALL,
    )(hot, x, *after)


def frozen_body(parts, more, source_ref, *rest):
    row_refs, weight_refs, out_ref = rest[:parts], rest[parts : 2 * parts], rest[-1]
    total = rest[2 * parts][...] if more else jnp.zeros(out_ref.shape, F32)
    for q in range(parts):
        total += lax.dot_general(
            row_refs[q][...],
            weight_refs[q][...],
            (((1,), (1,)), ((), ())),
            preferred_element_type=F32,
        )
    out_ref[...] = total


def frozen_product(sources, row_blocks, weights, so_far, *after):
    parts = len(row_blocks)
    rows, features = row_blocks[0].shape
    inputs = weights.shape[0]
    nb = 512 if inputs % 512 == 0 else inputs

    def columns(q):
        return pl.BlockSpec((nb, features), lambda n, source: (n, source[q]))

    more = () if so_far is None else (so_far,)
    out_spec = pl.BlockSpec((rows, nb), lambda n, source: (0, n))
    return pl.pallas_call(
        functools.partial(frozen_body, parts, so_far is not None),
        grid_spec=pltpu.PrefetchScalarGridSpec(
            num_scalar_prefetch=1,
            grid=(inputs // nb,),
            in_specs=[WHOLE] * parts
            + [columns(q) for q in range(parts)]
            + [out_spec] * len(more)
            + [ANY] * len(after),
            out_specs=out_spec,
        ),
        out_shape=jax.ShapeDtypeStruct((rows, inputs), F32),
        compiler_params=params(24 if more else VMEM_LIMIT),
        cost_estimate=SMALL,
    )(sources, *row_blocks, *([weights] * parts), *more, *after)


def receive_body(groups, windows, piece, table_ref, *rest):
    sent_refs = rest[:groups]
    out_ref, pick_ref, lane_ref, rows_ref, wide_ref, pick_one, lane_one, total_ref = rest[-8:]
    slots, top, _ = table_ref.shape
    count = windows * piece
    step = pl.program_id(0)

    def place(s):
        source = lax.rem(lax.axis_index("grp") + groups - s, groups)
        return pl.ds(pl.multiple_of(source * count, 8), count)

    @pl.when(step == 0)
    def _():
        column = lax.broadcasted_iota(jnp.int32, (piece, top), 1).astype(F32)
        for s in range(groups):
            notes = sent_refs[s][:, :128].astype(F32)[count:]
            for at in range(windows):
                limit = notes[1:2, at : at + 1]
                rows = slice(at * piece, (at + 1) * piece)
                lane_one[rows, :] = jnp.where(
                    column < limit, (top // 8) / jnp.maximum(limit, 1.0), 0.0
                )
                pick_one[rows, :] = jnp.broadcast_to(notes[0:1, at : at + 1], (piece, top))
            lane_ref[place(s), :] = lane_one[...]
            pick_ref[place(s), :] = pick_one[...]
        total_ref[...] = jnp.zeros_like(total_ref)

    for s in range(groups):
        wide_ref[place(s), :] = sent_refs[s][...].astype(F32)[:count]
    rows = wide_ref[...].astype(BF16)
    rows_ref[...] = rows
    total_ref[...] += lax.dot_general(
        rows,
        table_ref[...].reshape(slots * top, table_ref.shape[2]),
        (((1,), (1,)), ((), ())),
        preferred_element_type=F32,
    )

    @pl.when(step == pl.num_programs(0) - 1)
    def _():
        out_ref[...] = choose(pick_ref, total_ref, slots)


def choose(pick_ref, total_ref, slots):
    top = pick_ref.shape[1]
    chosen = total_ref[:, :top]
    for e in range(1, slots):
        chosen = jnp.where(
            pick_ref[...] == float(e), total_ref[:, e * top : (e + 1) * top], chosen
        )
    return chosen


def receive(sent, table, windows, piece, *after):
    groups = len(sent)
    slots, top, features = table.shape
    count = windows * piece
    rows = groups * count
    fb = feature_block(features)
    fixed = pl.BlockSpec((rows, top), lambda f: (0, 0))
    return pl.pallas_call(
        functools.partial(receive_body, groups, windows, piece),
        grid=(features // fb,),
        out_shape=[jax.ShapeDtypeStruct((rows, top), F32)] * 3
        + [jax.ShapeDtypeStruct((rows, features), BF16)],
        in_specs=[pl.BlockSpec((slots, top, fb), lambda f: (0, 0, f))]
        + [pl.BlockSpec((count + NOTES, fb), lambda f: (0, f))] * groups
        + [ANY] * len(after),
        out_specs=[fixed] * 3 + [pl.BlockSpec((rows, fb), lambda f: (0, f))],
        scratch_shapes=[
            pltpu.VMEM((rows, fb), F32),
            pltpu.VMEM((count, top), F32),
            pltpu.VMEM((count, top), F32),
            pltpu.VMEM((rows, slots * top), F32),
        ],
        compiler_params=params(24),
        cost_estimate=SMALL,
    )(table, *sent, *after)


def project_body(groups, pick_ref, table_ref, *rest):
    out_ref, rows_ref, wide_ref, total_ref = rest[-4:]
    slots = table_ref.shape[0]
    step = pl.program_id(0)

    @pl.when(step == 0)
    def _():
        total_ref[...] = jnp.zeros_like(total_ref)

    rows = by_group(wide_ref, rest[:groups], -1)
    rows_ref[...] = rows
    table = jnp.concatenate([table_ref[e] for e in range(slots)], axis=1)
    total_ref[...] += jnp.dot(rows, table, preferred_element_type=F32)

    @pl.when(step == pl.num_programs(0) - 1)
    def _():
        out_ref[...] = choose(pick_ref, total_ref, slots)


def project(blocks, pick, table, *after):
    count, top = pick.shape
    groups = len(blocks)
    slots, features = table.shape[:2]
    fb = feature_block(features)
    return pl.pallas_call(
        functools.partial(project_body, groups),
        grid=(features // fb,),
        out_shape=[
            jax.ShapeDtypeStruct((count, top), F32),
            jax.ShapeDtypeStruct((count, features), BF16),
        ],
        in_specs=[WHOLE, pl.BlockSpec((slots, fb, top), lambda f: (0, f, 0))]
        + [pl.BlockSpec((count // groups, fb), lambda f: (0, f))] * groups
        + [ANY] * len(after),
        out_specs=[
            pl.BlockSpec((count, top), lambda f: (0, 0)),
            pl.BlockSpec((count, fb), lambda f: (0, f)),
        ],
        scratch_shapes=[
            pltpu.VMEM((count, fb), F32),
            pltpu.VMEM((count, slots * top), F32),
        ],
        compiler_params=params(24),
        cost_estimate=SMALL,
    )(pick, table, *blocks, *after)


def spread(values, pick, slots):
    return jnp.concatenate(
        [jnp.where(pick == float(e), values, 0.0) for e in range(slots)], axis=1
    ).astype(BF16)


def back_body(groups, mine_ref, other_ref, lane_ref, pick_ref, down_ref, *rest):
    out_refs, spread_ref, wide_ref = rest[-2 - groups : -2], rest[-2], rest[-1]
    slots, width, top = down_ref.shape

    @pl.when(pl.program_id(0) == 0)
    def _():
        lowered = ((mine_ref[...] + other_ref[...]) * lane_ref[...]).astype(BF16).astype(F32)
        spread_ref[...] = spread(lowered, pick_ref[...], slots)

    table = jnp.concatenate([down_ref[e] for e in range(slots)], axis=1)
    wide_ref[...] = lax.dot_general(
        spread_ref[...], table, (((1,), (1,)), ((), ())), preferred_element_type=F32
    )
    by_shift(out_refs, wide_ref, -1)


def back(mine, other, lane, pick, down, groups, *after):
    rows, top = pick.shape
    slots, features, _ = down.shape
    fb = feature_block(features)
    each = rows // groups
    return pl.pallas_call(
        functools.partial(back_body, groups),
        grid=(features // fb,),
        out_shape=[jax.ShapeDtypeStruct((each, features), BF16)] * groups
        + [jax.ShapeDtypeStruct((rows, slots * top), BF16)],
        in_specs=[WHOLE] * 4
        + [pl.BlockSpec((slots, fb, top), lambda f: (0, f, 0))]
        + [ANY] * len(after),
        out_specs=[pl.BlockSpec((each, fb), lambda f: (0, f))] * groups
        + [pl.BlockSpec((rows, slots * top), lambda f: (0, 0))],
        scratch_shapes=[pltpu.VMEM((rows, fb), F32)],
        compiler_params=params(24),
        cost_estimate=SMALL,
    )(mine, other, lane, pick, down, *after)


def grads_body(
    slots,
    mine_ref,
    other_ref,
    lane_ref,
    pick_ref,
    low_ref,
    acts_ref,
    masked_ref,
    *rest,
):
    down_ref, up_ref, largest_ref, lift_ref = rest[-4:]
    top = lane_ref.shape[1]

    @pl.when(pl.program_id(0) == 0)
    def _():
        lifted = ((mine_ref[...] + other_ref[...]) * lane_ref[...]).astype(BF16).astype(F32)
        for e in range(slots):
            part = jnp.where(pick_ref[...] == float(e), lifted, 0.0)
            lift_ref[e * top : (e + 1) * top, :] = part.T.astype(BF16)
        largest_ref[...] = jnp.zeros_like(largest_ref)

    up = jnp.dot(lift_ref[...], masked_ref[...], preferred_element_type=F32)
    down = lax.dot_general(
        acts_ref[...], low_ref[...], (((0,), (0,)), ((), ())), preferred_element_type=F32
    )
    for e in range(slots):
        up_ref[e] = up[e * top : (e + 1) * top]
        down_ref[e] = down[:, e * top : (e + 1) * top]
    top_up = jnp.max(jnp.abs(up).reshape(slots * top // 8, 8, up.shape[1]), axis=0)
    top_down = jnp.max(jnp.abs(down).reshape(down.shape[0] // 8, 8, slots * top), axis=0)
    largest = largest_ref[...]
    for c in range(up.shape[1] // top):
        largest = jnp.maximum(largest, top_up[:, c * top : (c + 1) * top])
    for e in range(slots):
        largest = jnp.maximum(largest, top_down[:, e * top : (e + 1) * top])
    largest_ref[...] = largest


def grads(mine, other, lane, pick, low, acts, masked, slots, *after):
    rows, top = pick.shape
    features = acts.shape[1]
    fb = feature_block(features)
    return pl.pallas_call(
        functools.partial(grads_body, slots),
        grid=(features // fb,),
        out_shape=[
            jax.ShapeDtypeStruct((slots, features, top), F32),
            jax.ShapeDtypeStruct((slots, top, features), F32),
            jax.ShapeDtypeStruct((8, top), F32),
        ],
        in_specs=[WHOLE] * 5
        + [pl.BlockSpec((rows, fb), lambda f: (0, f))] * 2
        + [ANY] * len(after),
        out_specs=[
            pl.BlockSpec((slots, fb, top), lambda f: (0, f, 0)),
            pl.BlockSpec((slots, top, fb), lambda f: (0, 0, f)),
            pl.BlockSpec((8, top), lambda f: (0, 0)),
        ],
        scratch_shapes=[pltpu.VMEM((slots * top, rows), BF16)],
        compiler_params=params(28),
        cost_estimate=SMALL,
    )(mine, other, lane, pick, low, acts, masked, *after)


def scaled_body(largest_ref, down_ref, up_ref, down_out, up_out):
    highest = jnp.max(largest_ref[...], keepdims=True)
    factor = grad_limit / jnp.maximum(highest, grad_limit)
    for e in range(down_ref.shape[0]):
        down_out[e] = (down_ref[e] * factor).astype(BF16)
        up_out[e] = (up_ref[e] * factor).astype(BF16)


def scaled(largest, down, up):
    slots, features, top = down.shape
    down_spec = pl.BlockSpec((1, features, top), lambda e: (e, 0, 0))
    up_spec = pl.BlockSpec((1, top, features), lambda e: (e, 0, 0))
    return pl.pallas_call(
        scaled_body,
        grid=(slots,),
        out_shape=[
            jax.ShapeDtypeStruct(down.shape, BF16),
            jax.ShapeDtypeStruct(up.shape, BF16),
        ],
        in_specs=[WHOLE, down_spec, up_spec],
        out_specs=[down_spec, up_spec],
        compiler_params=params(16),
        cost_estimate=SMALL,
    )(largest, down, up)


def finish_body(groups, hot_ref, frozen_ref, *rest):
    out_ref, wide_ref = rest[-2:]
    own = jnp.dot(
        hot_ref[...], by_group(wide_ref, rest[:groups], 1), preferred_element_type=F32
    )
    out_ref[...] = (frozen_ref[...] + own).astype(BF16)


def finish(hot, frozen, returned):
    groups = len(returned)
    native, features = frozen.shape
    each = returned[0].shape[0]
    fb = feature_block(features)
    return pl.pallas_call(
        functools.partial(finish_body, groups),
        grid=(features // fb,),
        out_shape=jax.ShapeDtypeStruct((native, features), BF16),
        in_specs=[WHOLE, pl.BlockSpec((native, fb), lambda f: (0, f))]
        + [pl.BlockSpec((each, fb), lambda f: (0, f))] * groups,
        out_specs=pl.BlockSpec((native, fb), lambda f: (0, f)),
        scratch_shapes=[pltpu.VMEM((groups * each, fb), F32)],
        compiler_params=params(24),
        cost_estimate=SMALL,
    )(hot, frozen, *returned)


def partner(x, axis, bit):
    count = lax.axis_size(axis)
    return lax.ppermute(x, axis, [(i, i ^ bit) for i in range(count)])


def all_but_last_sum(near_first, x, axis):
    count = lax.axis_size(axis)
    bits = [bit for bit in (1 << i for i in range(count.bit_length())) if bit < count]
    for bit in bits[:-1] if near_first else bits[:0:-1]:
        x = x + partner(x, axis, bit)
    return x, partner(x, axis, bits[-1] if near_first else bits[0])


def gather_rows(x):
    count = lax.axis_size("tp")
    me = lax.axis_index("tp").astype(jnp.int32)
    near = jnp.stack([me, me ^ 1]), [x, partner(x, "tp", 1)]
    sources, blocks = [], []
    for step in range(2, count, 2):
        far = lax.ppermute(x, "tp", [(i, (i + step) % count) for i in range(count)])
        blocks.append(far)
        sources.append((me - step) % count)
    return near, ((jnp.stack(sources), blocks) if blocks else None)


def all_max(x, axis):
    count = lax.axis_size(axis)
    bit = 1
    while bit < count:
        x = jnp.maximum(x, partner(x, axis, bit))
        bit *= 2
    return x


def local(
    activations,
    cotangent,
    frozen_weight_matrix,
    adapter_down_weights,
    adapter_up_weights,
    window_adapter,
    window_live_rows,
    rank_per_adapter,
    slot_per_adapter,
):
    groups = lax.axis_size("grp")
    slots, features, top = adapter_down_weights.shape
    micro, windows, piece, _ = activations.shape

    def native(x):
        return x.transpose(0, 2, 1, 3).reshape(micro * piece * windows, features)

    def across(blocks, sign):
        return [blocks[0]] + [
            lax.ppermute(blocks[s], "grp", [(i, (i + sign * s) % groups) for i in range(groups)])
            for s in range(1, groups)
        ]

    *masked_out, masked_flat, hot = route(
        native(cotangent),
        window_adapter,
        slot_per_adapter,
        rank_per_adapter,
        window_live_rows,
        groups,
        slots,
    )
    masked_sent = across(masked_out, 1)
    near, far = gather_rows(masked_flat)
    frozen = frozen_product(*near, frozen_weight_matrix, None, masked_sent[1])
    *acts_out, hot_back = pack(native(activations), hot, groups, masked_sent[3], frozen)
    acts_sent = across(acts_out, 1)
    low_part, pick, lane, masked = receive(
        masked_sent, adapter_up_weights, micro * WINDOWS_PER_OWNER, piece, frozen
    )

    def lower(near_first, low_part, pick, lane, table, far, weights, frozen):
        low_mine, low_other = all_but_last_sum(near_first, low_part, "tp")
        if far:
            frozen = frozen_product(*far, weights, frozen, low_part)
        *backs, low = back(low_mine, low_other, lane, pick, table, groups, frozen)
        return backs, low, frozen

    def lift(near_first, acts_sent, low, pick, lane, masked, table, far, weights, frozen):
        lift_part, acts = project(acts_sent, pick, table, low)
        lift_mine, lift_other = all_but_last_sum(near_first, lift_part, "tp")
        if far:
            sources, blocks = far
            blocks = [partner(x, "tp", 1) for x in blocks]
            frozen = frozen_product(sources ^ 1, blocks, weights, frozen, lift_part)
        down_sum, up_sum, largest = grads(
            lift_mine, lift_other, lane, pick, low, acts, masked, slots, frozen
        )
        largest = all_max(all_max(largest, "tp"), "grp")
        return scaled(largest, down_sum, up_sum), frozen

    early = window_live_rows[0, 0] <= piece
    backs, low, frozen = lax.cond(
        early,
        functools.partial(lower, True),
        functools.partial(lower, False),
        low_part,
        pick,
        lane,
        adapter_down_weights,
        far,
        frozen_weight_matrix,
        frozen,
    )
    returned = across(backs, -1)
    (grad_down, grad_up), frozen = lax.cond(
        early,
        functools.partial(lift, True),
        functools.partial(lift, False),
        acts_sent,
        low,
        pick,
        lane,
        masked,
        adapter_down_weights,
        far,
        frozen_weight_matrix,
        frozen,
    )
    input_grad = finish(hot_back, frozen, returned)
    return (
        input_grad.reshape(micro, piece, windows, features).transpose(0, 2, 1, 3),
        grad_down,
        grad_up,
    )


def solution(mesh):
    return jax.shard_map(
        local,
        mesh=mesh,
        in_specs=(
            P("rep", "grp", None, "tp"),
            P("rep", "grp", None, "tp"),
            P("tp", None),
            P(("rep", "grp"), "tp", None),
            P(("rep", "grp"), None, "tp"),
            P("rep", "grp"),
            P("rep", "grp"),
            P("rep"),
            P("rep"),
        ),
        out_specs=(
            P("rep", "grp", None, "tp"),
            P(("rep", "grp"), "tp", None),
            P(("rep", "grp"), None, "tp"),
        ),
        check_vma=False,
    )
```

```python
import functools

import jax
import jax.numpy as jnp
from jax import lax
from jax.experimental import pallas as pl
from jax.experimental.pallas import tpu as pltpu
from jax.sharding import PartitionSpec as P

WINDOWS_PER_OWNER = 2
NOTES = 8

grad_limit = 4.0

BF16 = jnp.bfloat16
F32 = jnp.float32
VMEM_LIMIT = 60
WHOLE = pl.BlockSpec(memory_space=pltpu.VMEM)
ANY = pl.BlockSpec(memory_space=pl.ANY)


def params(limit=VMEM_LIMIT):
    return pltpu.CompilerParams(
        dimension_semantics=("arbitrary",), vmem_limit_bytes=limit * 1024 * 1024
    )


SMALL = pl.CostEstimate(flops=1000000, bytes_accessed=100000, transcendentals=0)


def feature_block(features, wanted=512):
    return wanted if features % wanted == 0 else features


def window_order(adapter_ref, slot_ref, order_ref, count_ref, groups, slots):
    micro, windows = adapter_ref.shape
    for m in range(micro):
        for o in range(groups):
            count_ref[o] = 0
            for k in range(WINDOWS_PER_OWNER):
                order_ref[(m * groups + o) * WINDOWS_PER_OWNER + k] = -1
        for j in range(windows):
            owner = lax.div(slot_ref[adapter_ref[m, j]], slots)
            k = jnp.minimum(count_ref[owner], WINDOWS_PER_OWNER - 1)
            order_ref[(m * groups + owner) * WINDOWS_PER_OWNER + k] = j
            count_ref[owner] = k + 1


def live_rows_native(live_ref, m, windows):
    sublane = lax.broadcasted_iota(jnp.int32, (windows, 128), 0)
    live = jnp.zeros((windows, 128), jnp.int32)
    for j in range(windows):
        live = jnp.where(sublane == j, live_ref[m, j], live)
    return live


def route_body(
    groups,
    slots,
    piece,
    adapter_in,
    slot_in,
    rank_in,
    live_in,
    x_ref,
    *rest,
):
    out_refs = rest[:groups]
    (
    flat_ref,
    hot_ref,
    adapter_ref,
    slot_ref,
    rank_ref,
    live_ref,
    arrived,
    order_ref,
    count_ref,
    target_ref,
    alive_ref,
    note_ref,
    packed_ref,
    ) = rest[groups:]
    micro, windows = adapter_ref.shape

    @pl.when(pl.program_id(0) == 0)
    def _():
        copies = [
            pltpu.make_async_copy(there, here, arrived.at[i])
            for i, (there, here) in enumerate(
                (
                    (adapter_in, adapter_ref),
                    (slot_in, slot_ref),
                    (rank_in, rank_ref),
                    (live_in, live_ref),
                )
            )
        ]
        for copy in copies:
            copy.start()
        for copy in copies:
            copy.wait()
        window_order(adapter_ref, slot_ref, order_ref, count_ref, groups, slots)
        row = lax.broadcasted_iota(jnp.int32, (piece, 128), 0)
        note_row = lax.broadcasted_iota(jnp.int32, (NOTES, 128), 0)
        note_column = lax.broadcasted_iota(jnp.int32, (NOTES, 128), 1)
        note_ref[...] = jnp.zeros_like(note_ref)
        for o in range(groups):
            note = jnp.zeros((NOTES, 128), jnp.int32)
            for m in range(micro):
                for k in range(WINDOWS_PER_OWNER):
                    j = order_ref[(m * groups + o) * WINDOWS_PER_OWNER + k]
                    at = jnp.maximum(j, 0)
                    adapter = adapter_ref[m, at]
                    live = jnp.where(j >= 0, live_ref[m, at], 0)
                    limit = jnp.where(j >= 0, rank_ref[adapter], 0)
                    first = ((o * micro + m) * WINDOWS_PER_OWNER + k) * piece
                    target_ref[first : first + piece, :] = jnp.where(
                        row < live, (m * piece + row) * windows + j, -1
                    )
                    value = jnp.where(note_row == 0, lax.rem(slot_ref[adapter], slots), limit)
                    note = jnp.where(note_column == m * WINDOWS_PER_OWNER + k, value, note)
            note_ref[o, :, :128] = note.astype(F32)
        column = lax.broadcasted_iota(jnp.int32, hot_ref.shape, 1)
        hot_ref[...] = jnp.where(column == target_ref[:, :1], 1.0, 0.0).astype(BF16)
        for m in range(micro):
            live = live_rows_native(live_ref, m, windows)
            for p in range(piece):
                first = (m * piece + p) * windows
                alive_ref[first : first + windows, :] = jnp.where(live > p, 1.0, 0.0)

    x = x_ref[...]
    packed = jnp.dot(hot_ref[...], x, preferred_element_type=F32)
    rows = packed.shape[0] // groups
    parts = []
    for o in range(groups):
        parts += [packed[o * rows : (o + 1) * rows], note_ref[o]]
    packed_ref[...] = jnp.concatenate(parts, axis=0)
    for s in range(groups):
        owner = lax.rem(lax.axis_index("grp") + s, groups)
        first = pl.multiple_of(owner * (rows + NOTES), 8)
        out_refs[s][...] = packed_ref[pl.ds(first, rows + NOTES), :].astype(BF16)
    flat_ref[...] = jnp.where(alive_ref[:, :1] > 0.0, x.astype(F32), 0.0).astype(BF16)


def route(x, adapter, slot_per_adapter, rank_per_adapter, live, groups, slots):
    micro, windows = adapter.shape
    native, features = x.shape
    piece = native // (micro * windows)
    rows = groups * micro * WINDOWS_PER_OWNER * piece
    sent = rows // groups + NOTES
    fb = feature_block(features, 1024)
    far = pl.BlockSpec(memory_space=pltpu.MemorySpace.HBM)
    return pl.pallas_call(
        functools.partial(route_body, groups, slots, piece),
        grid=(features // fb,),
        out_shape=[jax.ShapeDtypeStruct((sent, features), BF16)] * groups
        + [
            jax.ShapeDtypeStruct((native, features), BF16),
            jax.ShapeDtypeStruct((rows, native), BF16),
        ],
        in_specs=[far] * 4 + [pl.BlockSpec((native, fb), lambda f: (0, f))],
        out_specs=[pl.BlockSpec((sent, fb), lambda f: (0, f))] * groups
        + [
            pl.BlockSpec((native, fb), lambda f: (0, f)),
            pl.BlockSpec((rows, native), lambda f: (0, 0)),
        ],
        scratch_shapes=[
            pltpu.SMEM(adapter.shape, jnp.int32),
            pltpu.SMEM(slot_per_adapter.shape, jnp.int32),
            pltpu.SMEM(rank_per_adapter.shape, jnp.int32),
            pltpu.SMEM(live.shape, jnp.int32),
            pltpu.SemaphoreType.DMA((4,)),
            pltpu.SMEM((micro * groups * WINDOWS_PER_OWNER,), jnp.int32),
            pltpu.SMEM((groups,), jnp.int32),
            pltpu.VMEM((rows, 128), jnp.int32),
            pltpu.VMEM((native, 128), F32),
            pltpu.VMEM((groups, NOTES, fb), F32),
            pltpu.VMEM((groups * sent, fb), F32),
        ],
        compiler_params=params(),
        cost_estimate=SMALL,
    )(adapter, slot_per_adapter, rank_per_adapter, live, x)


def by_shift(out_refs, wide_ref, sign):
    groups = len(out_refs)
    rows = out_refs[0].shape[0]
    for s in range(groups):
        group = lax.rem(lax.axis_index("grp") + groups + sign * s, groups)
        here = pl.ds(pl.multiple_of(group * rows, 8), rows)
        out_refs[s][...] = wide_ref[here, :].astype(BF16)


def by_group(wide_ref, in_refs, sign):
    groups = len(in_refs)
    rows = in_refs[0].shape[0]
    for s in range(groups):
        group = lax.rem(lax.axis_index("grp") + groups + sign * s, groups)
        here = pl.ds(pl.multiple_of(group * rows, 8), rows)
        wide_ref[here, :] = in_refs[s][...].astype(F32)
    return wide_ref[...].astype(BF16)


def pack_body(groups, hot_ref, x_ref, *rest):
    out_refs, hot_back_ref, wide_ref = rest[-2 - groups : -2], rest[-2], rest[-1]

    @pl.when(pl.program_id(0) == 0)
    def _():
        hot_back_ref[...] = hot_ref[...].astype(F32).T.astype(BF16)

    wide_ref[...] = jnp.dot(hot_ref[...], x_ref[...], preferred_element_type=F32)
    by_shift(out_refs, wide_ref, 1)


def pack(x, hot, groups, *after):
    native, features = x.shape
    rows = hot.shape[0]
    fb = feature_block(features, 1024)
    return pl.pallas_call(
        functools.partial(pack_body, groups),
        grid=(features // fb,),
        out_shape=[jax.ShapeDtypeStruct((rows // groups, features), BF16)] * groups
        + [jax.ShapeDtypeStruct((native, rows), BF16)],
        in_specs=[WHOLE, pl.BlockSpec((native, fb), lambda f: (0, f))] + [ANY] * len(after),
        out_specs=[pl.BlockSpec((rows // groups, fb), lambda f: (0, f))] * groups
        + [pl.BlockSpec((native, rows), lambda f: (0, 0))],
        scratch_shapes=[pltpu.VMEM((rows, fb), F32)],
        compiler_params=params(),
        cost_estimate=SMALL,
    )(hot, x, *after)


def frozen_body(parts, more, source_ref, *rest):
    row_refs, weight_refs, out_ref = rest[:parts], rest[parts : 2 * parts], rest[-1]
    total = rest[2 * parts][...] if more else jnp.zeros(out_ref.shape, F32)
    for q in range(parts):
        total += lax.dot_general(
            row_refs[q][...],
            weight_refs[q][...],
            (((1,), (1,)), ((), ())),
            preferred_element_type=F32,
        )
    out_ref[...] = total


def frozen_product(sources, row_blocks, weights, so_far, *after):
    parts = len(row_blocks)
    rows, features = row_blocks[0].shape
    inputs = weights.shape[0]
    nb = 512 if inputs % 512 == 0 else inputs

    def columns(q):
        return pl.BlockSpec((nb, features), lambda n, source: (n, source[q]))

    more = () if so_far is None else (so_far,)
    out_spec = pl.BlockSpec((rows, nb), lambda n, source: (0, n))
    return pl.pallas_call(
        functools.partial(frozen_body, parts, so_far is not None),
        grid_spec=pltpu.PrefetchScalarGridSpec(
            num_scalar_prefetch=1,
            grid=(inputs // nb,),
            in_specs=[WHOLE] * parts
            + [columns(q) for q in range(parts)]
            + [out_spec] * len(more)
            + [ANY] * len(after),
            out_specs=out_spec,
        ),
        out_shape=jax.ShapeDtypeStruct((rows, inputs), F32),
        compiler_params=params(24 if more else VMEM_LIMIT),
        cost_estimate=SMALL,
    )(sources, *row_blocks, *([weights] * parts), *more, *after)


def receive_body(groups, windows, piece, table_ref, *rest):
    sent_refs = rest[:groups]
    out_ref, pick_ref, lane_ref, rows_ref, wide_ref, pick_one, lane_one, total_ref = rest[-8:]
    slots, top, _ = table_ref.shape
    count = windows * piece
    step = pl.program_id(0)

    def place(s):
        source = lax.rem(lax.axis_index("grp") + groups - s, groups)
        return pl.ds(pl.multiple_of(source * count, 8), count)

    @pl.when(step == 0)
    def _():
        column = lax.broadcasted_iota(jnp.int32, (piece, top), 1).astype(F32)
        for s in range(groups):
            notes = sent_refs[s][:, :128].astype(F32)[count:]
            for at in range(windows):
                limit = notes[1:2, at : at + 1]
                rows = slice(at * piece, (at + 1) * piece)
                lane_one[rows, :] = jnp.where(
                    column < limit, (top // 8) / jnp.maximum(limit, 1.0), 0.0
                )
                pick_one[rows, :] = jnp.broadcast_to(notes[0:1, at : at + 1], (piece, top))
            lane_ref[place(s), :] = lane_one[...]
            pick_ref[place(s), :] = pick_one[...]
        total_ref[...] = jnp.zeros_like(total_ref)

    for s in range(groups):
        wide_ref[place(s), :] = sent_refs[s][...].astype(F32)[:count]
    rows = wide_ref[...].astype(BF16)
    rows_ref[...] = rows
    total_ref[...] += lax.dot_general(
        rows,
        table_ref[...].reshape(slots * top, table_ref.shape[2]),
        (((1,), (1,)), ((), ())),
        preferred_element_type=F32,
    )

    @pl.when(step == pl.num_programs(0) - 1)
    def _():
        out_ref[...] = choose(pick_ref, total_ref, slots)


def choose(pick_ref, total_ref, slots):
    top = pick_ref.shape[1]
    chosen = total_ref[:, :top]
    for e in range(1, slots):
        chosen = jnp.where(
            pick_ref[...] == float(e), total_ref[:, e * top : (e + 1) * top], chosen
        )
    return chosen


def receive(sent, table, windows, piece, *after):
    groups = len(sent)
    slots, top, features = table.shape
    count = windows * piece
    rows = groups * count
    fb = feature_block(features)
    fixed = pl.BlockSpec((rows, top), lambda f: (0, 0))
    return pl.pallas_call(
        functools.partial(receive_body, groups, windows, piece),
        grid=(features // fb,),
        out_shape=[jax.ShapeDtypeStruct((rows, top), F32)] * 3
        + [jax.ShapeDtypeStruct((rows, features), BF16)],
        in_specs=[pl.BlockSpec((slots, top, fb), lambda f: (0, 0, f))]
        + [pl.BlockSpec((count + NOTES, fb), lambda f: (0, f))] * groups
        + [ANY] * len(after),
        out_specs=[fixed] * 3 + [pl.BlockSpec((rows, fb), lambda f: (0, f))],
        scratch_shapes=[
            pltpu.VMEM((rows, fb), F32),
            pltpu.VMEM((count, top), F32),
            pltpu.VMEM((count, top), F32),
            pltpu.VMEM((rows, slots * top), F32),
        ],
        compiler_params=params(24),
        cost_estimate=SMALL,
    )(table, *sent, *after)


def gate_body(*refs):
    pass


def gate(blocks, *after):
    return pl.pallas_call(
        gate_body,
        out_shape=[jax.ShapeDtypeStruct(x.shape, x.dtype) for x in blocks],
        in_specs=[ANY] * (len(blocks) + len(after)),
        out_specs=[ANY] * len(blocks),
        input_output_aliases={i: i for i in range(len(blocks))},
        cost_estimate=SMALL,
    )(*blocks, *after)


def project_body(groups, pick_ref, table_ref, *rest):
    out_ref, rows_ref, wide_ref, total_ref = rest[-4:]
    slots = table_ref.shape[0]
    step = pl.program_id(0)

    @pl.when(step == 0)
    def _():
        total_ref[...] = jnp.zeros_like(total_ref)

    rows = by_group(wide_ref, rest[:groups], -1)
    rows_ref[...] = rows
    table = jnp.concatenate([table_ref[e] for e in range(slots)], axis=1)
    total_ref[...] += jnp.dot(rows, table, preferred_element_type=F32)

    @pl.when(step == pl.num_programs(0) - 1)
    def _():
        out_ref[...] = choose(pick_ref, total_ref, slots)


def project(blocks, pick, table, *after):
    count, top = pick.shape
    groups = len(blocks)
    slots, features = table.shape[:2]
    fb = feature_block(features, 1024)
    return pl.pallas_call(
        functools.partial(project_body, groups),
        grid=(features // fb,),
        out_shape=[
            jax.ShapeDtypeStruct((count, top), F32),
            jax.ShapeDtypeStruct((count, features), BF16),
        ],
        in_specs=[WHOLE, pl.BlockSpec((slots, fb, top), lambda f: (0, f, 0))]
        + [pl.BlockSpec((count // groups, fb), lambda f: (0, f))] * groups
        + [ANY] * len(after),
        out_specs=[
            pl.BlockSpec((count, top), lambda f: (0, 0)),
            pl.BlockSpec((count, fb), lambda f: (0, f)),
        ],
        scratch_shapes=[
            pltpu.VMEM((count, fb), F32),
            pltpu.VMEM((count, slots * top), F32),
        ],
        compiler_params=params(24),
        cost_estimate=SMALL,
    )(pick, table, *blocks, *after)


def spread(values, pick, slots):
    return jnp.concatenate(
        [jnp.where(pick == float(e), values, 0.0) for e in range(slots)], axis=1
    ).astype(BF16)


def back_body(groups, mine_ref, other_ref, lane_ref, pick_ref, down_ref, *rest):
    out_refs, spread_ref, wide_ref = rest[-2 - groups : -2], rest[-2], rest[-1]
    slots, width, top = down_ref.shape

    @pl.when(pl.program_id(0) == 0)
    def _():
        lowered = ((mine_ref[...] + other_ref[...]) * lane_ref[...]).astype(BF16).astype(F32)
        spread_ref[...] = spread(lowered, pick_ref[...], slots)

    table = jnp.concatenate([down_ref[e] for e in range(slots)], axis=1)
    wide_ref[...] = lax.dot_general(
        spread_ref[...], table, (((1,), (1,)), ((), ())), preferred_element_type=F32
    )
    by_shift(out_refs, wide_ref, -1)


def back(mine, other, lane, pick, down, groups, *after):
    rows, top = pick.shape
    slots, features, _ = down.shape
    fb = feature_block(features, 1024)
    each = rows // groups
    return pl.pallas_call(
        functools.partial(back_body, groups),
        grid=(features // fb,),
        out_shape=[jax.ShapeDtypeStruct((each, features), BF16)] * groups
        + [jax.ShapeDtypeStruct((rows, slots * top), BF16)],
        in_specs=[WHOLE] * 4
        + [pl.BlockSpec((slots, fb, top), lambda f: (0, f, 0))]
        + [ANY] * len(after),
        out_specs=[pl.BlockSpec((each, fb), lambda f: (0, f))] * groups
        + [pl.BlockSpec((rows, slots * top), lambda f: (0, 0))],
        scratch_shapes=[pltpu.VMEM((rows, fb), F32)],
        compiler_params=params(24),
        cost_estimate=SMALL,
    )(mine, other, lane, pick, down, *after)


def grads_body(
    slots,
    mine_ref,
    other_ref,
    lane_ref,
    pick_ref,
    low_ref,
    acts_ref,
    masked_ref,
    *rest,
):
    down_ref, up_ref, largest_ref, lift_ref = rest[-4:]
    top = lane_ref.shape[1]

    @pl.when(pl.program_id(0) == 0)
    def _():
        lifted = ((mine_ref[...] + other_ref[...]) * lane_ref[...]).astype(BF16).astype(F32)
        for e in range(slots):
            part = jnp.where(pick_ref[...] == float(e), lifted, 0.0)
            lift_ref[e * top : (e + 1) * top, :] = part.T.astype(BF16)
        largest_ref[...] = jnp.zeros_like(largest_ref)

    up = jnp.dot(lift_ref[...], masked_ref[...], preferred_element_type=F32)
    down = lax.dot_general(
        acts_ref[...], low_ref[...], (((0,), (0,)), ((), ())), preferred_element_type=F32
    )
    for e in range(slots):
        up_ref[e] = up[e * top : (e + 1) * top]
        down_ref[e] = down[:, e * top : (e + 1) * top]
    top_up = jnp.max(jnp.abs(up).reshape(slots * top // 8, 8, up.shape[1]), axis=0)
    top_down = jnp.max(jnp.abs(down).reshape(down.shape[0] // 8, 8, slots * top), axis=0)
    largest = largest_ref[...]
    for c in range(up.shape[1] // top):
        largest = jnp.maximum(largest, top_up[:, c * top : (c + 1) * top])
    for e in range(slots):
        largest = jnp.maximum(largest, top_down[:, e * top : (e + 1) * top])
    largest_ref[...] = largest


def grads(mine, other, lane, pick, low, acts, masked, slots, *after):
    rows, top = pick.shape
    features = acts.shape[1]
    fb = feature_block(features, 1024)
    return pl.pallas_call(
        functools.partial(grads_body, slots),
        grid=(features // fb,),
        out_shape=[
            jax.ShapeDtypeStruct((slots, features, top), F32),
            jax.ShapeDtypeStruct((slots, top, features), F32),
            jax.ShapeDtypeStruct((8, top), F32),
        ],
        in_specs=[WHOLE] * 5
        + [pl.BlockSpec((rows, fb), lambda f: (0, f))] * 2
        + [ANY] * len(after),
        out_specs=[
            pl.BlockSpec((slots, fb, top), lambda f: (0, f, 0)),
            pl.BlockSpec((slots, top, fb), lambda f: (0, 0, f)),
            pl.BlockSpec((8, top), lambda f: (0, 0)),
        ],
        scratch_shapes=[pltpu.VMEM((slots * top, rows), BF16)],
        compiler_params=params(28),
        cost_estimate=SMALL,
    )(mine, other, lane, pick, low, acts, masked, *after)


def scaled_body(largest_ref, down_ref, up_ref, down_out, up_out):
    highest = jnp.max(largest_ref[...], keepdims=True)
    factor = grad_limit / jnp.maximum(highest, grad_limit)
    for e in range(down_ref.shape[0]):
        down_out[e] = (down_ref[e] * factor).astype(BF16)
        up_out[e] = (up_ref[e] * factor).astype(BF16)


def scaled(largest, down, up):
    slots, features, top = down.shape
    down_spec = pl.BlockSpec((2, features, top), lambda e: (e, 0, 0))
    up_spec = pl.BlockSpec((2, top, features), lambda e: (e, 0, 0))
    return pl.pallas_call(
        scaled_body,
        grid=(slots // 2,),
        out_shape=[
            jax.ShapeDtypeStruct(down.shape, BF16),
            jax.ShapeDtypeStruct(up.shape, BF16),
        ],
        in_specs=[WHOLE, down_spec, up_spec],
        out_specs=[down_spec, up_spec],
        compiler_params=params(32),
        cost_estimate=SMALL,
    )(largest, down, up)


def finish_body(groups, hot_ref, frozen_ref, *rest):
    out_ref, wide_ref = rest[-2:]
    own = jnp.dot(
        hot_ref[...], by_group(wide_ref, rest[:groups], 1), preferred_element_type=F32
    )
    out_ref[...] = (frozen_ref[...] + own).astype(BF16)


def finish(hot, frozen, returned):
    groups = len(returned)
    native, features = frozen.shape
    each = returned[0].shape[0]
    fb = feature_block(features, 1024)
    return pl.pallas_call(
        functools.partial(finish_body, groups),
        grid=(features // fb,),
        out_shape=jax.ShapeDtypeStruct((native, features), BF16),
        in_specs=[WHOLE, pl.BlockSpec((native, fb), lambda f: (0, f))]
        + [pl.BlockSpec((each, fb), lambda f: (0, f))] * groups,
        out_specs=pl.BlockSpec((native, fb), lambda f: (0, f)),
        scratch_shapes=[pltpu.VMEM((groups * each, fb), F32)],
        compiler_params=params(24),
        cost_estimate=SMALL,
    )(hot, frozen, *returned)


def partner(x, axis, bit):
    count = lax.axis_size(axis)
    return lax.ppermute(x, axis, [(i, i ^ bit) for i in range(count)])


def all_but_last_sum(near_first, x, axis):
    count = lax.axis_size(axis)
    bits = [bit for bit in (1 << i for i in range(count.bit_length())) if bit < count]
    for bit in bits[:-1] if near_first else bits[:0:-1]:
        x = x + partner(x, axis, bit)
    return x, partner(x, axis, bits[-1] if near_first else bits[0])


def gather_rows(x):
    count = lax.axis_size("tp")
    me = lax.axis_index("tp").astype(jnp.int32)
    near = jnp.stack([me, me ^ 1]), [x, partner(x, "tp", 1)]
    sources, blocks = [], []
    for step in range(2, count, 2):
        far = lax.ppermute(x, "tp", [(i, (i + step) % count) for i in range(count)])
        blocks.append(far)
        sources.append((me - step) % count)
    return near, ((jnp.stack(sources), blocks) if blocks else None)


def all_max(x, axis):
    count = lax.axis_size(axis)
    bit = 1
    while bit < count:
        x = jnp.maximum(x, partner(x, axis, bit))
        bit *= 2
    return x


def local(
    activations,
    cotangent,
    frozen_weight_matrix,
    adapter_down_weights,
    adapter_up_weights,
    window_adapter,
    window_live_rows,
    rank_per_adapter,
    slot_per_adapter,
):
    groups = lax.axis_size("grp")
    slots, features, top = adapter_down_weights.shape
    micro, windows, piece, _ = activations.shape

    def native(x):
        return x.transpose(0, 2, 1, 3).reshape(micro * piece * windows, features)

    def across(blocks, sign):
        return [blocks[0]] + [
            lax.ppermute(blocks[s], "grp", [(i, (i + sign * s) % groups) for i in range(groups)])
            for s in range(1, groups)
        ]

    *masked_out, masked_flat, hot = route(
        native(cotangent),
        window_adapter,
        slot_per_adapter,
        rank_per_adapter,
        window_live_rows,
        groups,
        slots,
    )
    masked_sent = across(masked_out, 1)
    near, far = gather_rows(masked_flat)
    frozen = frozen_product(*near, frozen_weight_matrix, None, masked_sent[1])
    *acts_out, hot_back = pack(native(activations), hot, groups, masked_sent[3], frozen)
    acts_sent = across(acts_out, 1)
    low_part, pick, lane, masked = receive(
        masked_sent, adapter_up_weights, micro * WINDOWS_PER_OWNER, piece, frozen
    )

    def lower(near_first, low_part, pick, lane, table):
        low_mine, low_other = all_but_last_sum(near_first, low_part, "tp")
        *backs, low = back(low_mine, low_other, lane, pick, table, groups)
        return backs, low

    def lift(near_first, acts_sent, low, pick, lane, masked, table, far, weights, frozen):
        lift_part, acts = project(acts_sent, pick, table, low)
        lift_mine, lift_other = all_but_last_sum(near_first, lift_part, "tp")
        if far:
            sources = jnp.concatenate([far[0], far[0] ^ 1])
            blocks = far[1] + [partner(x, "tp", 1) for x in far[1]]
            frozen = frozen_product(sources, blocks, weights, frozen, lift_part)
        down_sum, up_sum, largest = grads(
            lift_mine, lift_other, lane, pick, low, acts, masked, slots, frozen
        )
        largest = all_max(all_max(largest, "tp"), "grp")
        return scaled(largest, down_sum, up_sum), frozen

    early = window_live_rows[0, 0] <= piece
    backs, low = lax.cond(
        early,
        functools.partial(lower, True),
        functools.partial(lower, False),
        low_part,
        pick,
        lane,
        adapter_down_weights,
    )
    returned = across(gate(backs, acts_sent[2]), -1)
    (grad_down, grad_up), frozen = lax.cond(
        early,
        functools.partial(lift, True),
        functools.partial(lift, False),
        acts_sent,
        low,
        pick,
        lane,
        masked,
        adapter_down_weights,
        far,
        frozen_weight_matrix,
        frozen,
    )
    input_grad = finish(hot_back, frozen, returned)
    return (
        input_grad.reshape(micro, piece, windows, features).transpose(0, 2, 1, 3),
        grad_down,
        grad_up,
    )


def solution(mesh):
    return jax.shard_map(
        local,
        mesh=mesh,
        in_specs=(
            P("rep", "grp", None, "tp"),
            P("rep", "grp", None, "tp"),
            P("tp", None),
            P(("rep", "grp"), "tp", None),
            P(("rep", "grp"), None, "tp"),
            P("rep", "grp"),
            P("rep", "grp"),
            P("rep"),
            P("rep"),
        ),
        out_specs=(
            P("rep", "grp", None, "tp"),
            P(("rep", "grp"), "tp", None),
            P(("rep", "grp"), None, "tp"),
        ),
        check_vma=False,
    )
```

```python
import functools

import jax
import jax.numpy as jnp
from jax import lax
from jax.experimental import pallas as pl
from jax.experimental.pallas import tpu as pltpu
from jax.sharding import PartitionSpec as P

WINDOWS_PER_OWNER = 2
NOTES = 8

grad_limit = 4.0

BF16 = jnp.bfloat16
F32 = jnp.float32
VMEM_LIMIT = 60
WHOLE = pl.BlockSpec(memory_space=pltpu.VMEM)
ANY = pl.BlockSpec(memory_space=pl.ANY)


def params(limit=VMEM_LIMIT):
    return pltpu.CompilerParams(
        dimension_semantics=("arbitrary",), vmem_limit_bytes=limit * 1024 * 1024
    )


SMALL = pl.CostEstimate(flops=1000000, bytes_accessed=100000, transcendentals=0)


def feature_block(features, wanted=512):
    return wanted if features % wanted == 0 else features


def window_order(adapter_ref, slot_ref, order_ref, count_ref, groups, slots):
    micro, windows = adapter_ref.shape
    for m in range(micro):
        for o in range(groups):
            count_ref[o] = 0
            for k in range(WINDOWS_PER_OWNER):
                order_ref[(m * groups + o) * WINDOWS_PER_OWNER + k] = -1
        for j in range(windows):
            owner = lax.div(slot_ref[adapter_ref[m, j]], slots)
            k = jnp.minimum(count_ref[owner], WINDOWS_PER_OWNER - 1)
            order_ref[(m * groups + owner) * WINDOWS_PER_OWNER + k] = j
            count_ref[owner] = k + 1


def live_rows_native(live_ref, m, windows):
    sublane = lax.broadcasted_iota(jnp.int32, (windows, 128), 0)
    live = jnp.zeros((windows, 128), jnp.int32)
    for j in range(windows):
        live = jnp.where(sublane == j, live_ref[m, j], live)
    return live


def route_body(
    groups,
    slots,
    piece,
    adapter_in,
    slot_in,
    rank_in,
    live_in,
    x_ref,
    *rest,
):
    out_refs = rest[:groups]
    (
    flat_ref,
    hot_ref,
    adapter_ref,
    slot_ref,
    rank_ref,
    live_ref,
    arrived,
    order_ref,
    count_ref,
    target_ref,
    alive_ref,
    note_ref,
    packed_ref,
    ) = rest[groups:]
    micro, windows = adapter_ref.shape

    @pl.when(pl.program_id(0) == 0)
    def _():
        copies = [
            pltpu.make_async_copy(there, here, arrived.at[i])
            for i, (there, here) in enumerate(
                (
                    (adapter_in, adapter_ref),
                    (slot_in, slot_ref),
                    (rank_in, rank_ref),
                    (live_in, live_ref),
                )
            )
        ]
        for copy in copies:
            copy.start()
        for copy in copies:
            copy.wait()
        window_order(adapter_ref, slot_ref, order_ref, count_ref, groups, slots)
        row = lax.broadcasted_iota(jnp.int32, (piece, 128), 0)
        note_row = lax.broadcasted_iota(jnp.int32, (NOTES, 128), 0)
        note_column = lax.broadcasted_iota(jnp.int32, (NOTES, 128), 1)
        note_ref[...] = jnp.zeros_like(note_ref)
        for o in range(groups):
            note = jnp.zeros((NOTES, 128), jnp.int32)
            for m in range(micro):
                for k in range(WINDOWS_PER_OWNER):
                    j = order_ref[(m * groups + o) * WINDOWS_PER_OWNER + k]
                    at = jnp.maximum(j, 0)
                    adapter = adapter_ref[m, at]
                    live = jnp.where(j >= 0, live_ref[m, at], 0)
                    limit = jnp.where(j >= 0, rank_ref[adapter], 0)
                    first = ((o * micro + m) * WINDOWS_PER_OWNER + k) * piece
                    target_ref[first : first + piece, :] = jnp.where(
                        row < live, (m * piece + row) * windows + j, -1
                    )
                    value = jnp.where(note_row == 0, lax.rem(slot_ref[adapter], slots), limit)
                    note = jnp.where(note_column == m * WINDOWS_PER_OWNER + k, value, note)
            note_ref[o, :, :128] = note.astype(F32)
        column = lax.broadcasted_iota(jnp.int32, hot_ref.shape, 1)
        hot_ref[...] = jnp.where(column == target_ref[:, :1], 1.0, 0.0).astype(BF16)
        for m in range(micro):
            live = live_rows_native(live_ref, m, windows)
            for p in range(piece):
                first = (m * piece + p) * windows
                alive_ref[first : first + windows, :] = jnp.where(live > p, 1.0, 0.0)

    x = x_ref[...]
    packed = jnp.dot(hot_ref[...], x, preferred_element_type=F32)
    rows = packed.shape[0] // groups
    parts = []
    for o in range(groups):
        parts += [packed[o * rows : (o + 1) * rows], note_ref[o]]
    packed_ref[...] = jnp.concatenate(parts, axis=0)
    for s in range(groups):
        owner = lax.rem(lax.axis_index("grp") + s, groups)
        first = pl.multiple_of(owner * (rows + NOTES), 8)
        out_refs[s][...] = packed_ref[pl.ds(first, rows + NOTES), :].astype(BF16)
    flat_ref[...] = jnp.where(alive_ref[:, :1] > 0.0, x.astype(F32), 0.0).astype(BF16)


def route(x, adapter, slot_per_adapter, rank_per_adapter, live, groups, slots):
    micro, windows = adapter.shape
    native, features = x.shape
    piece = native // (micro * windows)
    rows = groups * micro * WINDOWS_PER_OWNER * piece
    sent = rows // groups + NOTES
    fb = feature_block(features, 1024)
    far = pl.BlockSpec(memory_space=pltpu.MemorySpace.HBM)
    return pl.pallas_call(
        functools.partial(route_body, groups, slots, piece),
        grid=(features // fb,),
        out_shape=[jax.ShapeDtypeStruct((sent, features), BF16)] * groups
        + [
            jax.ShapeDtypeStruct((native, features), BF16),
            jax.ShapeDtypeStruct((rows, native), BF16),
        ],
        in_specs=[far] * 4 + [pl.BlockSpec((native, fb), lambda f: (0, f))],
        out_specs=[pl.BlockSpec((sent, fb), lambda f: (0, f))] * groups
        + [
            pl.BlockSpec((native, fb), lambda f: (0, f)),
            pl.BlockSpec((rows, native), lambda f: (0, 0)),
        ],
        scratch_shapes=[
            pltpu.SMEM(adapter.shape, jnp.int32),
            pltpu.SMEM(slot_per_adapter.shape, jnp.int32),
            pltpu.SMEM(rank_per_adapter.shape, jnp.int32),
            pltpu.SMEM(live.shape, jnp.int32),
            pltpu.SemaphoreType.DMA((4,)),
            pltpu.SMEM((micro * groups * WINDOWS_PER_OWNER,), jnp.int32),
            pltpu.SMEM((groups,), jnp.int32),
            pltpu.VMEM((rows, 128), jnp.int32),
            pltpu.VMEM((native, 128), F32),
            pltpu.VMEM((groups, NOTES, fb), F32),
            pltpu.VMEM((groups * sent, fb), F32),
        ],
        compiler_params=params(),
        cost_estimate=SMALL,
    )(adapter, slot_per_adapter, rank_per_adapter, live, x)


def by_shift(out_refs, wide_ref, sign):
    groups = len(out_refs)
    rows = out_refs[0].shape[0]
    for s in range(groups):
        group = lax.rem(lax.axis_index("grp") + groups + sign * s, groups)
        here = pl.ds(pl.multiple_of(group * rows, 8), rows)
        out_refs[s][...] = wide_ref[here, :].astype(BF16)


def by_group(wide_ref, in_refs, sign):
    groups = len(in_refs)
    rows = in_refs[0].shape[0]
    for s in range(groups):
        group = lax.rem(lax.axis_index("grp") + groups + sign * s, groups)
        here = pl.ds(pl.multiple_of(group * rows, 8), rows)
        wide_ref[here, :] = in_refs[s][...].astype(F32)
    return wide_ref[...].astype(BF16)


def pack_body(groups, hot_ref, x_ref, *rest):
    out_refs, hot_back_ref, wide_ref = rest[-2 - groups : -2], rest[-2], rest[-1]

    @pl.when(pl.program_id(0) == 0)
    def _():
        hot_back_ref[...] = hot_ref[...].astype(F32).T.astype(BF16)

    wide_ref[...] = jnp.dot(hot_ref[...], x_ref[...], preferred_element_type=F32)
    by_shift(out_refs, wide_ref, 1)


def pack(x, hot, groups, *after):
    native, features = x.shape
    rows = hot.shape[0]
    fb = feature_block(features, 1024)
    return pl.pallas_call(
        functools.partial(pack_body, groups),
        grid=(features // fb,),
        out_shape=[jax.ShapeDtypeStruct((rows // groups, features), BF16)] * groups
        + [jax.ShapeDtypeStruct((native, rows), BF16)],
        in_specs=[WHOLE, pl.BlockSpec((native, fb), lambda f: (0, f))] + [ANY] * len(after),
        out_specs=[pl.BlockSpec((rows // groups, fb), lambda f: (0, f))] * groups
        + [pl.BlockSpec((native, rows), lambda f: (0, 0))],
        scratch_shapes=[pltpu.VMEM((rows, fb), F32)],
        compiler_params=params(),
        cost_estimate=SMALL,
    )(hot, x, *after)


def frozen_body(parts, more, source_ref, *rest):
    row_refs, weight_refs, out_ref = rest[:parts], rest[parts : 2 * parts], rest[-1]
    total = rest[2 * parts][...] if more else jnp.zeros(out_ref.shape, F32)
    for q in range(parts):
        total += lax.dot_general(
            row_refs[q][...],
            weight_refs[q][...],
            (((1,), (1,)), ((), ())),
            preferred_element_type=F32,
        )
    out_ref[...] = total


def frozen_product(sources, row_blocks, weights, so_far, *after):
    parts = len(row_blocks)
    rows, features = row_blocks[0].shape
    inputs = weights.shape[0]
    nb = 512 if inputs % 512 == 0 else inputs

    def columns(q):
        return pl.BlockSpec((nb, features), lambda n, source: (n, source[q]))

    more = () if so_far is None else (so_far,)
    out_spec = pl.BlockSpec((rows, nb), lambda n, source: (0, n))
    return pl.pallas_call(
        functools.partial(frozen_body, parts, so_far is not None),
        grid_spec=pltpu.PrefetchScalarGridSpec(
            num_scalar_prefetch=1,
            grid=(inputs // nb,),
            in_specs=[WHOLE] * parts
            + [columns(q) for q in range(parts)]
            + [out_spec] * len(more)
            + [ANY] * len(after),
            out_specs=out_spec,
        ),
        out_shape=jax.ShapeDtypeStruct((rows, inputs), F32),
        compiler_params=params(24 if more else VMEM_LIMIT),
        cost_estimate=SMALL,
    )(sources, *row_blocks, *([weights] * parts), *more, *after)


def receive_body(groups, windows, piece, table_ref, *rest):
    sent_refs = rest[:groups]
    out_ref, pick_ref, lane_ref, rows_ref, wide_ref, pick_one, lane_one, total_ref = rest[-8:]
    slots, top, _ = table_ref.shape
    count = windows * piece
    step = pl.program_id(0)

    def place(s):
        source = lax.rem(lax.axis_index("grp") + groups - s, groups)
        return pl.ds(pl.multiple_of(source * count, 8), count)

    @pl.when(step == 0)
    def _():
        column = lax.broadcasted_iota(jnp.int32, (piece, top), 1).astype(F32)
        for s in range(groups):
            notes = sent_refs[s][:, :128].astype(F32)[count:]
            for at in range(windows):
                limit = notes[1:2, at : at + 1]
                rows = slice(at * piece, (at + 1) * piece)
                lane_one[rows, :] = jnp.where(
                    column < limit, (top // 8) / jnp.maximum(limit, 1.0), 0.0
                )
                pick_one[rows, :] = jnp.broadcast_to(notes[0:1, at : at + 1], (piece, top))
            lane_ref[place(s), :] = lane_one[...]
            pick_ref[place(s), :] = pick_one[...]
        total_ref[...] = jnp.zeros_like(total_ref)

    for s in range(groups):
        wide_ref[place(s), :] = sent_refs[s][...].astype(F32)[:count]
    rows = wide_ref[...].astype(BF16)
    rows_ref[...] = rows
    total_ref[...] += lax.dot_general(
        rows,
        table_ref[...].reshape(slots * top, table_ref.shape[2]),
        (((1,), (1,)), ((), ())),
        preferred_element_type=F32,
    )

    @pl.when(step == pl.num_programs(0) - 1)
    def _():
        out_ref[...] = choose(pick_ref, total_ref, slots)


def choose(pick_ref, total_ref, slots):
    top = pick_ref.shape[1]
    chosen = total_ref[:, :top]
    for e in range(1, slots):
        chosen = jnp.where(
            pick_ref[...] == float(e), total_ref[:, e * top : (e + 1) * top], chosen
        )
    return chosen


def receive(sent, table, windows, piece, *after):
    groups = len(sent)
    slots, top, features = table.shape
    count = windows * piece
    rows = groups * count
    fb = feature_block(features, 1024)
    fixed = pl.BlockSpec((rows, top), lambda f: (0, 0))
    return pl.pallas_call(
        functools.partial(receive_body, groups, windows, piece),
        grid=(features // fb,),
        out_shape=[jax.ShapeDtypeStruct((rows, top), F32)] * 3
        + [jax.ShapeDtypeStruct((rows, features), BF16)],
        in_specs=[pl.BlockSpec((slots, top, fb), lambda f: (0, 0, f))]
        + [pl.BlockSpec((count + NOTES, fb), lambda f: (0, f))] * groups
        + [ANY] * len(after),
        out_specs=[fixed] * 3 + [pl.BlockSpec((rows, fb), lambda f: (0, f))],
        scratch_shapes=[
            pltpu.VMEM((rows, fb), F32),
            pltpu.VMEM((count, top), F32),
            pltpu.VMEM((count, top), F32),
            pltpu.VMEM((rows, slots * top), F32),
        ],
        compiler_params=params(24),
        cost_estimate=SMALL,
    )(table, *sent, *after)


def gate_body(*refs):
    pass


def gate(blocks, *after):
    return pl.pallas_call(
        gate_body,
        out_shape=[jax.ShapeDtypeStruct(x.shape, x.dtype) for x in blocks],
        in_specs=[ANY] * (len(blocks) + len(after)),
        out_specs=[ANY] * len(blocks),
        input_output_aliases={i: i for i in range(len(blocks))},
        cost_estimate=SMALL,
    )(*blocks, *after)


def project_body(groups, pick_ref, table_ref, *rest):
    out_ref, rows_ref, wide_ref, total_ref = rest[-4:]
    slots = table_ref.shape[0]
    step = pl.program_id(0)

    @pl.when(step == 0)
    def _():
        total_ref[...] = jnp.zeros_like(total_ref)

    rows = by_group(wide_ref, rest[:groups], -1)
    rows_ref[...] = rows
    table = jnp.concatenate([table_ref[e] for e in range(slots)], axis=1)
    total_ref[...] += jnp.dot(rows, table, preferred_element_type=F32)

    @pl.when(step == pl.num_programs(0) - 1)
    def _():
        out_ref[...] = choose(pick_ref, total_ref, slots)


def project(blocks, pick, table, *after):
    count, top = pick.shape
    groups = len(blocks)
    slots, features = table.shape[:2]
    fb = feature_block(features, 1024)
    return pl.pallas_call(
        functools.partial(project_body, groups),
        grid=(features // fb,),
        out_shape=[
            jax.ShapeDtypeStruct((count, top), F32),
            jax.ShapeDtypeStruct((count, features), BF16),
        ],
        in_specs=[WHOLE, pl.BlockSpec((slots, fb, top), lambda f: (0, f, 0))]
        + [pl.BlockSpec((count // groups, fb), lambda f: (0, f))] * groups
        + [ANY] * len(after),
        out_specs=[
            pl.BlockSpec((count, top), lambda f: (0, 0)),
            pl.BlockSpec((count, fb), lambda f: (0, f)),
        ],
        scratch_shapes=[
            pltpu.VMEM((count, fb), F32),
            pltpu.VMEM((count, slots * top), F32),
        ],
        compiler_params=params(24),
        cost_estimate=SMALL,
    )(pick, table, *blocks, *after)


def spread(values, pick, slots):
    return jnp.concatenate(
        [jnp.where(pick == float(e), values, 0.0) for e in range(slots)], axis=1
    ).astype(BF16)


def back_body(groups, mine_ref, other_ref, lane_ref, pick_ref, down_ref, *rest):
    out_refs, spread_ref, wide_ref = rest[-2 - groups : -2], rest[-2], rest[-1]
    slots, width, top = down_ref.shape

    @pl.when(pl.program_id(0) == 0)
    def _():
        lowered = ((mine_ref[...] + other_ref[...]) * lane_ref[...]).astype(BF16).astype(F32)
        spread_ref[...] = spread(lowered, pick_ref[...], slots)

    table = jnp.concatenate([down_ref[e] for e in range(slots)], axis=1)
    wide_ref[...] = lax.dot_general(
        spread_ref[...], table, (((1,), (1,)), ((), ())), preferred_element_type=F32
    )
    by_shift(out_refs, wide_ref, -1)


def back(mine, other, lane, pick, down, groups, *after):
    rows, top = pick.shape
    slots, features, _ = down.shape
    fb = feature_block(features, 1024)
    each = rows // groups
    return pl.pallas_call(
        functools.partial(back_body, groups),
        grid=(features // fb,),
        out_shape=[jax.ShapeDtypeStruct((each, features), BF16)] * groups
        + [jax.ShapeDtypeStruct((rows, slots * top), BF16)],
        in_specs=[WHOLE] * 4
        + [pl.BlockSpec((slots, fb, top), lambda f: (0, f, 0))]
        + [ANY] * len(after),
        out_specs=[pl.BlockSpec((each, fb), lambda f: (0, f))] * groups
        + [pl.BlockSpec((rows, slots * top), lambda f: (0, 0))],
        scratch_shapes=[pltpu.VMEM((rows, fb), F32)],
        compiler_params=params(24),
        cost_estimate=SMALL,
    )(mine, other, lane, pick, down, *after)


def grads_body(
    slots,
    mine_ref,
    other_ref,
    lane_ref,
    pick_ref,
    low_ref,
    acts_ref,
    masked_ref,
    *rest,
):
    down_ref, up_ref, largest_ref, lift_ref = rest[-4:]
    top = lane_ref.shape[1]

    @pl.when(pl.program_id(0) == 0)
    def _():
        lifted = ((mine_ref[...] + other_ref[...]) * lane_ref[...]).astype(BF16).astype(F32)
        for e in range(slots):
            part = jnp.where(pick_ref[...] == float(e), lifted, 0.0)
            lift_ref[e * top : (e + 1) * top, :] = part.T.astype(BF16)
        largest_ref[...] = jnp.zeros_like(largest_ref)

    up = jnp.dot(lift_ref[...], masked_ref[...], preferred_element_type=F32)
    down = lax.dot_general(
        acts_ref[...], low_ref[...], (((0,), (0,)), ((), ())), preferred_element_type=F32
    )
    for e in range(slots):
        up_ref[e] = up[e * top : (e + 1) * top]
        down_ref[e] = down[:, e * top : (e + 1) * top]
    top_up = jnp.max(jnp.abs(up).reshape(slots * top // 8, 8, up.shape[1]), axis=0)
    top_down = jnp.max(jnp.abs(down).reshape(down.shape[0] // 8, 8, slots * top), axis=0)
    largest = largest_ref[...]
    for c in range(up.shape[1] // top):
        largest = jnp.maximum(largest, top_up[:, c * top : (c + 1) * top])
    for e in range(slots):
        largest = jnp.maximum(largest, top_down[:, e * top : (e + 1) * top])
    largest_ref[...] = largest


def grads(mine, other, lane, pick, low, acts, masked, slots, *after):
    rows, top = pick.shape
    features = acts.shape[1]
    fb = feature_block(features, 1024)
    return pl.pallas_call(
        functools.partial(grads_body, slots),
        grid=(features // fb,),
        out_shape=[
            jax.ShapeDtypeStruct((slots, features, top), F32),
            jax.ShapeDtypeStruct((slots, top, features), F32),
            jax.ShapeDtypeStruct((8, top), F32),
        ],
        in_specs=[WHOLE] * 5
        + [pl.BlockSpec((rows, fb), lambda f: (0, f))] * 2
        + [ANY] * len(after),
        out_specs=[
            pl.BlockSpec((slots, fb, top), lambda f: (0, f, 0)),
            pl.BlockSpec((slots, top, fb), lambda f: (0, 0, f)),
            pl.BlockSpec((8, top), lambda f: (0, 0)),
        ],
        scratch_shapes=[pltpu.VMEM((slots * top, rows), BF16)],
        compiler_params=params(28),
        cost_estimate=SMALL,
    )(mine, other, lane, pick, low, acts, masked, *after)


def scaled_body(largest_ref, down_ref, up_ref, down_out, up_out):
    highest = jnp.max(largest_ref[...], keepdims=True)
    factor = grad_limit / jnp.maximum(highest, grad_limit)
    for e in range(down_ref.shape[0]):
        down_out[e] = (down_ref[e] * factor).astype(BF16)
        up_out[e] = (up_ref[e] * factor).astype(BF16)


def scaled(largest, down, up):
    slots, features, top = down.shape
    down_spec = pl.BlockSpec((2, features, top), lambda e: (e, 0, 0))
    up_spec = pl.BlockSpec((2, top, features), lambda e: (e, 0, 0))
    return pl.pallas_call(
        scaled_body,
        grid=(slots // 2,),
        out_shape=[
            jax.ShapeDtypeStruct(down.shape, BF16),
            jax.ShapeDtypeStruct(up.shape, BF16),
        ],
        in_specs=[WHOLE, down_spec, up_spec],
        out_specs=[down_spec, up_spec],
        compiler_params=params(32),
        cost_estimate=SMALL,
    )(largest, down, up)


def finish_body(groups, hot_ref, frozen_ref, *rest):
    out_ref, wide_ref = rest[-2:]
    own = jnp.dot(
        hot_ref[...], by_group(wide_ref, rest[:groups], 1), preferred_element_type=F32
    )
    out_ref[...] = (frozen_ref[...] + own).astype(BF16)


def finish(hot, frozen, returned):
    groups = len(returned)
    native, features = frozen.shape
    each = returned[0].shape[0]
    fb = feature_block(features, 1024)
    return pl.pallas_call(
        functools.partial(finish_body, groups),
        grid=(features // fb,),
        out_shape=jax.ShapeDtypeStruct((native, features), BF16),
        in_specs=[WHOLE, pl.BlockSpec((native, fb), lambda f: (0, f))]
        + [pl.BlockSpec((each, fb), lambda f: (0, f))] * groups,
        out_specs=pl.BlockSpec((native, fb), lambda f: (0, f)),
        scratch_shapes=[pltpu.VMEM((groups * each, fb), F32)],
        compiler_params=params(24),
        cost_estimate=SMALL,
    )(hot, frozen, *returned)


def partner(x, axis, bit):
    count = lax.axis_size(axis)
    return lax.ppermute(x, axis, [(i, i ^ bit) for i in range(count)])


def all_but_last_sum(near_first, x, axis):
    count = lax.axis_size(axis)
    bits = [bit for bit in (1 << i for i in range(count.bit_length())) if bit < count]
    for bit in bits[:-1] if near_first else bits[:0:-1]:
        x = x + partner(x, axis, bit)
    return x, partner(x, axis, bits[-1] if near_first else bits[0])


def gather_rows(x):
    count = lax.axis_size("tp")
    me = lax.axis_index("tp").astype(jnp.int32)
    near = jnp.stack([me, me ^ 1]), [x, partner(x, "tp", 1)]
    sources, blocks = [], []
    for step in range(2, count, 2):
        far = lax.ppermute(x, "tp", [(i, (i + step) % count) for i in range(count)])
        blocks.append(far)
        sources.append((me - step) % count)
    return near, ((jnp.stack(sources), blocks) if blocks else None)


def all_max(x, axis):
    count = lax.axis_size(axis)
    bit = 1
    while bit < count:
        x = jnp.maximum(x, partner(x, axis, bit))
        bit *= 2
    return x


def local(
    activations,
    cotangent,
    frozen_weight_matrix,
    adapter_down_weights,
    adapter_up_weights,
    window_adapter,
    window_live_rows,
    rank_per_adapter,
    slot_per_adapter,
):
    groups = lax.axis_size("grp")
    slots, features, top = adapter_down_weights.shape
    micro, windows, piece, _ = activations.shape

    def native(x):
        return x.transpose(0, 2, 1, 3).reshape(micro * piece * windows, features)

    def across(blocks, sign):
        order = sorted(range(1, groups), key=lambda s: abs(2 * s - groups), reverse=sign > 0)
        moved = {0: blocks[0]}
        for s in order:
            pairs = [(i, (i + sign * s) % groups) for i in range(groups)]
            moved[s] = lax.ppermute(blocks[s], "grp", pairs)
        return [moved[s] for s in range(groups)]

    *masked_out, masked_flat, hot = route(
        native(cotangent),
        window_adapter,
        slot_per_adapter,
        rank_per_adapter,
        window_live_rows,
        groups,
        slots,
    )
    masked_sent = across(masked_out, 1)
    near, far = gather_rows(masked_flat)
    frozen = frozen_product(*near, frozen_weight_matrix, None, masked_sent[1])
    *acts_out, hot_back = pack(native(activations), hot, groups, masked_sent[3], frozen)
    acts_sent = across(acts_out, 1)
    low_part, pick, lane, masked = receive(
        masked_sent, adapter_up_weights, micro * WINDOWS_PER_OWNER, piece, frozen
    )

    def lower(near_first, low_part, pick, lane, table):
        low_mine, low_other = all_but_last_sum(near_first, low_part, "tp")
        *backs, low = back(low_mine, low_other, lane, pick, table, groups)
        return backs, low

    def lift(near_first, acts_sent, low, pick, lane, masked, table, far, weights, frozen):
        lift_part, acts = project(acts_sent, pick, table, low)
        lift_mine, lift_other = all_but_last_sum(near_first, lift_part, "tp")
        if far:
            sources = jnp.concatenate([far[0], far[0] ^ 1])
            blocks = far[1] + [partner(x, "tp", 1) for x in far[1]]
            frozen = frozen_product(sources, blocks, weights, frozen, lift_part)
        down_sum, up_sum, largest = grads(
            lift_mine, lift_other, lane, pick, low, acts, masked, slots, frozen
        )
        largest = all_max(all_max(largest, "tp"), "grp")
        return scaled(largest, down_sum, up_sum), frozen

    early = window_live_rows[0, 0] <= piece
    backs, low = lax.cond(
        early,
        functools.partial(lower, True),
        functools.partial(lower, False),
        low_part,
        pick,
        lane,
        adapter_down_weights,
    )
    returned = across(gate(backs, acts_sent[2]), -1)
    (grad_down, grad_up), frozen = lax.cond(
        early,
        functools.partial(lift, True),
        functools.partial(lift, False),
        acts_sent,
        low,
        pick,
        lane,
        masked,
        adapter_down_weights,
        far,
        frozen_weight_matrix,
        frozen,
    )
    input_grad = finish(hot_back, frozen, returned)
    return (
        input_grad.reshape(micro, piece, windows, features).transpose(0, 2, 1, 3),
        grad_down,
        grad_up,
    )


def solution(mesh):
    return jax.shard_map(
        local,
        mesh=mesh,
        in_specs=(
            P("rep", "grp", None, "tp"),
            P("rep", "grp", None, "tp"),
            P("tp", None),
            P(("rep", "grp"), "tp", None),
            P(("rep", "grp"), None, "tp"),
            P("rep", "grp"),
            P("rep", "grp"),
            P("rep"),
            P("rep"),
        ),
        out_specs=(
            P("rep", "grp", None, "tp"),
            P(("rep", "grp"), "tp", None),
            P(("rep", "grp"), None, "tp"),
        ),
        check_vma=False,
    )
```
